32 devices in a mesh: tm: 8 (over y, x, core), tile: 4 (over z).
Axes of the slice: x: 2, y: 2, z: 4, core: 2. Of those that a mesh axis runs over, the one named last changes fastest.
Arguments:
- queries: bfloat16 [4096, 1536], P(('tm', 'tile')), may hold values from -16 to 16
- keys: bfloat16 [4096, 1536], P(('tm', 'tile')), may hold values from -16 to 16
- values: bfloat16 [4096, 1536], P(('tm', 'tile')), may hold values from -6 to 6
- grad_out: bfloat16 [4096, 1536], P(('tm', 'tile')), may hold values from -6 to 6
- span_of_group: int32 [8], replicated, may hold values from 0 to 7, each once
- noise_level: int32 [8], replicated, may hold values from 0 to 999
- next_live: int32 [32], replicated, may hold values 0 or 1
- level_bias: float32 [1000, 12], replicated, may hold values from -2 to 2
Outputs:
- attended: bfloat16 [4096, 1536], P(('tm', 'tile'))
- grad_queries: bfloat16 [4096, 1536], P(('tm', 'tile'))
- grad_keys: bfloat16 [4096, 1536], P(('tm', 'tile'))
- grad_values: bfloat16 [4096, 1536], P(('tm', 'tile'))
The draws below stay inside these ranges and needn't reach their ends.
Inputs may be any that keep to these rules, and one draw needn't show every extreme that they name: span_of_group is a permutation of 0 to 7.
All inputs are finite; a program needn't handle non-finite values.
Results may differ from the reference program's by a relative error of at most 0.019.
Values may be sent and summed in bfloat16 or wider, within the bound.
No kernel may reach another device: no remote copies, remote signals or barrier semaphores. Data moves between devices by JAX's collectives and lax.ppermute only.
A program may use at most 256 MiB of HBM per device.

```python
import math
import jax
import jax.numpy as jnp
from jax import lax

D = 1536
H = 12
HD = 128
LEVELS = 1000
TOK_DEV = 128
TOKENS = 4096
N_TM = 8
N_TILE = 4


def shared_fields(key):
    base_keys = jax.random.normal(jax.random.fold_in(key, 11), (TOKENS, D), jnp.float32)
    base_queries = jax.random.normal(jax.random.fold_in(key, 12), (TOKENS, D), jnp.float32)
    return (jnp.clip(base_queries, -6.0, 6.0), jnp.clip(base_keys, -6.0, 6.0))


def draw_queries(key, part):
    return shared_fields(key)[0].astype(jnp.bfloat16)


def draw_keys(key, part):
    return shared_fields(key)[1].astype(jnp.bfloat16)


def plant(result, key, low, top_value):
    spot = [jax.random.randint(jax.random.fold_in(key, axis), (), 0, length) for axis, length in enumerate(result.shape)]
    widest = result.shape.index(max(result.shape))
    beside = spot[:widest] + [(spot[widest] + 1) % result.shape[widest]] + spot[widest + 1:]
    return result.at[tuple(spot)].set(low).at[tuple(beside)].set(top_value)


def levels(key, extent, pieces, smallest, largest):
    def one(dim, shards_of):
        steps = jax.random.uniform(jax.random.fold_in(jax.random.fold_in(key, 6), dim), (shards_of,), jnp.float32, smallest / len(pieces), largest / len(pieces))
        return jnp.repeat(jnp.exp(steps), extent[dim] // shards_of).reshape((-1,) + (1,) * (len(extent) - dim - 1))

    factor_of = one(*pieces[0])
    for cut in pieces[1:]:
        factor_of = factor_of * one(*cut)
    return factor_of


def noise(stream_key, extent, deviation, reach, cuts=(), held_as=jnp.bfloat16):
    drawn = jax.random.normal(stream_key, extent, jnp.float32) * deviation
    if len(cuts) > 0:
        drawn = levels(stream_key, extent, cuts, -0.22, 0.18) * drawn
    return jnp.clip(drawn, min=-reach, max=reach).astype(held_as)


def setup_inputs(seed: int = 0) -> dict:
    streams_of = jax.random.split(jax.random.key(seed), 9)
    return {
        "queries": draw_queries(jax.random.fold_in(streams_of[8], 71), 0),
        "keys": draw_keys(jax.random.fold_in(streams_of[8], 71), 0),
        "values": noise(streams_of[2], (TOKENS, D), 1.0, 6.0, ((0, 32),)),
        "grad_out": noise(streams_of[3], (TOKENS, D), 1.0, 6.0, ((0, 32),)),
        "span_of_group": jax.random.permutation(streams_of[4], N_TM).astype(jnp.int32),
        "noise_level": plant(jax.random.randint(streams_of[5], (N_TM,), 0, LEVELS), jax.random.fold_in(streams_of[5], 1), 0, LEVELS - 1).astype(jnp.int32),
        "next_live": plant((jax.random.randint(streams_of[6], (N_TM * N_TILE,), 0, 2) < 1).astype(jnp.int32), jax.random.fold_in(streams_of[6], 1), 0, 1),
        "level_bias": jnp.clip(jax.random.uniform(streams_of[7], (LEVELS, H), jnp.float32, -2.0, 2.0), -2.0, 2.0),
    }


def reference(queries, keys, values, grad_out, span_of_group, noise_level, next_live, level_bias):
    inv_root = 1.0 / math.sqrt(HD)
    cube_shape = (N_TM, N_TILE, TOK_DEV, H, HD)
    query_cube = queries.reshape(cube_shape)
    key_cube = keys.reshape(cube_shape)
    value_cube = values.reshape(cube_shape)
    grad_cube = grad_out.reshape(cube_shape)
    near_keys = jnp.concatenate([key_cube, jnp.roll(key_cube, -1, axis=1)], axis=2)
    near_values = jnp.concatenate([value_cube, jnp.roll(value_cube, -1, axis=1)], axis=2)
    group_bias = level_bias[noise_level[span_of_group]]
    live_table = next_live.reshape(N_TM, N_TILE)
    second_half = jnp.arange(2 * TOK_DEV) >= TOK_DEV

    def one_tile(grad_carry, flat_index):
        key_grads, value_grads = grad_carry
        group_no = flat_index // N_TILE
        tile_no = flat_index % N_TILE
        q_rows = query_cube[group_no, tile_no].astype(jnp.float32)
        k_rows = near_keys[:, tile_no].astype(jnp.float32)
        v_rows = near_values[:, tile_no].astype(jnp.float32)
        g_rows = grad_cube[group_no, tile_no].astype(jnp.float32)
        attend = span_of_group <= span_of_group[group_no]
        key_mask = attend[:, None] & (jnp.logical_not(second_half)[None, :] | (live_table[group_no, tile_no] == 1))
        scores = jnp.einsum('qhe,jkhe->jhqk', q_rows, k_rows) * inv_root + group_bias[:, :, None, None]
        scores = jnp.where(key_mask[:, None, None, :], scores, -1e+30)
        row_peak = lax.optimization_barrier(jnp.max(scores, axis=(0, 3)))
        log_total = row_peak + jnp.log(lax.optimization_barrier(jnp.sum(jnp.exp(scores - row_peak[None, :, :, None]), axis=(0, 3))))
        weights_full = jnp.exp(scores - log_total[None, :, :, None])
        weights_low = lax.optimization_barrier(weights_full.astype(jnp.bfloat16)).astype(jnp.float32)
        attended = jnp.einsum('jhqk,jkhe->qhe', weights_low, v_rows).astype(jnp.bfloat16)
        row_delta = lax.optimization_barrier(jnp.sum(g_rows * attended.astype(jnp.float32), axis=2)).T
        grad_weights = jnp.einsum('qhe,jkhe->jhqk', g_rows, v_rows)
        grad_scores = (weights_full * (grad_weights - row_delta[None, :, :, None]) * inv_root).astype(jnp.bfloat16)
        grad_scores = lax.optimization_barrier(grad_scores).astype(jnp.float32)
        grad_query = jnp.einsum('jhqk,jkhe->qhe', grad_scores, k_rows).astype(jnp.bfloat16)
        key_part = jnp.einsum('jhqk,qhe->jkhe', grad_scores, q_rows)
        value_part = jnp.einsum('jhqk,qhe->jkhe', weights_low, g_rows)
        key_grads = key_grads.at[:, tile_no].add(key_part)
        value_grads = value_grads.at[:, tile_no].add(value_part)
        return ((key_grads, value_grads), (attended, grad_query))
    zero_grads = jnp.zeros((N_TM, N_TILE, 2 * TOK_DEV, H, HD), jnp.float32)
    (key_grads, value_grads), (attended, grad_query) = lax.scan(one_tile, (zero_grads, zero_grads), jnp.arange(N_TM * N_TILE, dtype=jnp.int32))
    key_total = key_grads[:, :, :TOK_DEV] + jnp.roll(key_grads[:, :, TOK_DEV:], 1, axis=1)
    value_total = value_grads[:, :, :TOK_DEV] + jnp.roll(value_grads[:, :, TOK_DEV:], 1, axis=1)
    return (attended.reshape(TOKENS, D), grad_query.reshape(TOKENS, D), key_total.astype(jnp.bfloat16).reshape(TOKENS, D), value_total.astype(jnp.bfloat16).reshape(TOKENS, D))
```

```python
import functools
import math

import jax
import jax.numpy as jnp
from jax import lax
from jax.experimental import pallas as pl
from jax.experimental.pallas import tpu as pltpu
from jax.sharding import PartitionSpec as P

VMEM = pltpu.VMEM
SMEM = pltpu.SMEM
BF16 = jnp.bfloat16
F32 = jnp.float32
NT = (((1,), (1,)), ((), ()))
LOG2E = 1.4426950408889634


def params(mib):
    return pltpu.CompilerParams(vmem_limit_bytes=mib * 1024 * 1024)


def whole(space):
    return pl.BlockSpec(memory_space=space)


def shard_count(heads, groups):
    count = 1
    while heads % (2 * count) == 0 and groups % (2 * count) == 0:
        count *= 2
    return count


def pack_kernel(shards, width, pos_ref, q_ref, g_ref, k_ref, v_ref, *outs):
    shard = pos_ref[0]
    for hop in range(shards):
        lane = pl.multiple_of((shard ^ hop) * width, 128)
        full, pair = outs[hop], outs[shards + hop]
        full[0] = q_ref[:, pl.ds(lane, width)]
        full[1] = g_ref[:, pl.ds(lane, width)]
        k = k_ref[:, pl.ds(lane, width)]
        v = v_ref[:, pl.ds(lane, width)]
        full[2] = k
        full[3] = v
        pair[0] = k
        pair[1] = v


def attention_kernel(shards, replicas, tiles, inv_root, *refs):
    groups = shards * replicas
    slots = shards * replicas
    pos_ref, span_ref, live_ref, bias_ref = refs[:4]
    full = refs[4 : 4 + slots]
    ahead = refs[4 + slots : 4 + 2 * slots]
    outs = refs[4 + 2 * slots : 4 + 2 * slots + shards + replicas]
    rows_out, sums_out = outs[:shards], outs[shards:]
    ks, vs, kt, vt, dk, dv, prob = refs[4 + 2 * slots + shards + replicas :]
    tok = ks.shape[1] // 2
    local = pl.program_id(0)
    head = pos_ref[0] * pl.num_programs(0) + local
    shard, replica, tile = pos_ref[0], pos_ref[1], pos_ref[2]

    def group_of(turn, hop):
        return (shard ^ hop) * replicas + lax.rem(replica + turn, replicas)

    for turn in range(replicas):
        for hop in range(shards):
            slot = turn * shards + hop
            span = span_ref[group_of(turn, hop)]
            for plane, (k, v) in enumerate(
                ((full[slot][2], full[slot][3]), (ahead[slot][0], ahead[slot][1]))
            ):
                part = pl.ds(plane * tok, tok)
                ks[span, part, :] = k
                vs[span, part, :] = v
                kt[span, :, part] = k.T
                vt[span, :, part] = v.T
    dk[...] = jnp.zeros_like(dk)
    dv[...] = jnp.zeros_like(dv)

    def fold(op, x):
        return op(x.reshape(x.shape[0] // 8, 8, x.shape[1]), axis=0)

    def query_tile(hop, count, rows):
        q, g = full[hop][0], full[hop][1]
        scale = inv_root * LOG2E

        def score_step(i, peak):
            s = lax.dot_general(ks[i, :rows, :], q, NT, preferred_element_type=F32)
            s = s * scale + bias_ref[i, head] * LOG2E
            prob[i, :rows, :] = s
            return jnp.maximum(peak, fold(jnp.max, s))

        peak = lax.fori_loop(0, count, score_step, jnp.full((8, tok), -3e38, F32))
        peak = jnp.max(peak, axis=0, keepdims=True)

        def value_step(i, carry):
            total, out = carry
            e = jnp.exp2(prob[i, :rows, :] - peak)
            prob[i, :rows, :] = e
            total = total + fold(jnp.sum, e)
            out = out + jnp.dot(vt[i, :, :rows], e.astype(BF16), preferred_element_type=F32)
            return total, out

        total, out = lax.fori_loop(
            0, count, value_step, (jnp.zeros((8, tok), F32), jnp.zeros((q.shape[1], tok), F32))
        )
        inverse = 1.0 / jnp.sum(total, axis=0, keepdims=True)
        out = (out * inverse).astype(BF16)
        delta = jnp.sum(out.astype(F32) * g.T.astype(F32), axis=0, keepdims=True)
        rows_out[hop][0] = out.T

        def grad_step(i, dq):
            w = prob[i, :rows, :] * inverse
            dp = lax.dot_general(vs[i, :rows, :], g, NT, preferred_element_type=F32)
            ds = (w * (dp - delta) * inv_root).astype(BF16)
            dv[i, :rows, :] += jnp.dot(w.astype(BF16), g, preferred_element_type=F32)
            dk[i, :rows, :] += jnp.dot(ds, q, preferred_element_type=F32)
            return dq + jnp.dot(kt[i, :, :rows], ds, preferred_element_type=F32)

        dq = lax.fori_loop(0, count, grad_step, jnp.zeros((q.shape[1], tok), F32))
        rows_out[hop][1] = dq.astype(BF16).T

    for hop in range(shards):
        group = group_of(0, hop)
        count = span_ref[group] + 1
        live = live_ref[group * tiles + tile]

        @pl.when(live == 1)
        def _():
            query_tile(hop, count, 2 * tok)

        @pl.when(live != 1)
        def _():
            query_tile(hop, count, tok)

    for turn in range(replicas):
        for hop in range(shards):
            span = span_ref[group_of(turn, hop)]
            for plane in range(2):
                part = pl.ds(plane * tok, tok)
                sums_out[turn][hop, 2 * plane] = dk[span, part, :].astype(BF16)
                sums_out[turn][hop, 2 * plane + 1] = dv[span, part, :].astype(BF16)


def merge_kernel(shards, replicas, *refs):
    parts, outs = refs[:replicas], refs[replicas:]
    for hop in range(shards):
        for which in range(4):
            total = parts[0][hop, which].astype(F32)
            for part in parts[1:]:
                total = total + part[hop, which].astype(F32)
            outs[hop if which < 2 else shards + hop][which % 2] = total.astype(BF16)


def unpack_kernel(shards, width, pos_ref, *refs):
    rows, sums, ahead = refs[:shards], refs[shards : 2 * shards], refs[2 * shards : 3 * shards]
    out_ref, dq_ref, dk_ref, dv_ref = refs[3 * shards :]
    shard = pos_ref[0]
    for hop in range(shards):
        lanes = pl.ds(pl.multiple_of((shard ^ hop) * width, 128), width)
        out_ref[:, lanes] = rows[hop][0]
        dq_ref[:, lanes] = rows[hop][1]
        dk_ref[:, lanes] = (sums[hop][0].astype(F32) + ahead[hop][0].astype(F32)).astype(BF16)
        dv_ref[:, lanes] = (sums[hop][1].astype(F32) + ahead[hop][1].astype(F32)).astype(BF16)


def per_device(queries, keys, values, grad_out, span_of_group, noise_level, next_live, level_bias):
    tok, model = queries.shape
    heads = level_bias.shape[1]
    width = model // heads
    groups = lax.axis_size("tm")
    tiles = lax.axis_size("tile")
    shards = shard_count(heads, groups)
    replicas = groups // shards
    own_heads = heads // shards
    cols = own_heads * width
    inv_root = 1.0 / math.sqrt(width)
    me = lax.axis_index("tm")
    shard, replica = me // replicas, me % replicas
    pos = jnp.stack([shard, replica, lax.axis_index("tile")]).astype(jnp.int32)
    shape = jax.ShapeDtypeStruct

    def to_shard(x, hop, lift):
        if hop == 0 and lift == 0:
            return x
        pairs = []
        for t in range(groups):
            goal = ((t // replicas) ^ hop) * replicas + t % replicas
            for s in range(tiles):
                pairs.append((t * tiles + s, goal * tiles + (s + lift) % tiles))
        return lax.ppermute(x, ("tm", "tile"), pairs)

    def to_replica(x, turn):
        pairs = [(t, t // replicas * replicas + (t - turn) % replicas) for t in range(groups)]
        return lax.ppermute(x, "tm", pairs)

    packed = pl.pallas_call(
        functools.partial(pack_kernel, shards, cols),
        out_shape=[shape((4, tok, cols), BF16)] * shards + [shape((2, tok, cols), BF16)] * shards,
        in_specs=[whole(SMEM)] + [whole(VMEM)] * 4,
        out_specs=[whole(VMEM)] * (2 * shards),
        compiler_params=params(32),
        name="pack",
    )(pos, queries, grad_out, keys, values)
    full = [to_shard(packed[hop], hop, 0) for hop in range(shards)]
    ahead = [to_shard(packed[shards + hop], hop, -1) for hop in range(shards)]
    full_all, ahead_all = list(full), list(ahead)
    for turn in range(1, replicas):
        full_all += [to_replica(x, turn) for x in full]
        ahead_all += [to_replica(x, turn) for x in ahead]
    bias = level_bias.at[noise_level].get(mode="promise_in_bounds")

    def head_block(count):
        return pl.BlockSpec((count, tok, width), lambda h: (0, 0, h))

    stacked = pl.BlockSpec((shards, 4, tok, width), lambda h: (0, 0, 0, h))
    results = pl.pallas_call(
        functools.partial(attention_kernel, shards, replicas, tiles, inv_root),
        grid=(own_heads,),
        out_shape=[shape((2, tok, cols), BF16)] * shards
        + [shape((shards, 4, tok, cols), BF16)] * replicas,
        in_specs=[whole(SMEM)] * 4 + [head_block(4)] * groups + [head_block(2)] * groups,
        out_specs=[head_block(2)] * shards + [stacked] * replicas,
        scratch_shapes=[
            VMEM((groups, 2 * tok, width), BF16),
            VMEM((groups, 2 * tok, width), BF16),
            VMEM((groups, width, 2 * tok), BF16),
            VMEM((groups, width, 2 * tok), BF16),
            VMEM((groups, 2 * tok, width), F32),
            VMEM((groups, 2 * tok, width), F32),
            VMEM((groups, 2 * tok, tok), F32),
        ],
        compiler_params=params(48),
        name="attention",
    )(pos, span_of_group, next_live, bias, *full_all, *ahead_all)
    rows, sums = results[:shards], results[shards:]
    rows_home = [to_shard(rows[hop], hop, 0) for hop in range(shards)]
    parts = [sums[0]]
    for turn in range(1, replicas):
        parts.append(to_replica(sums[turn], replicas - turn))
    merged = pl.pallas_call(
        functools.partial(merge_kernel, shards, replicas),
        out_shape=[shape((2, tok, cols), BF16)] * (2 * shards),
        in_specs=[whole(VMEM)] * replicas,
        out_specs=[whole(VMEM)] * (2 * shards),
        compiler_params=params(48),
        name="merge",
    )(*parts)
    sums_home = [to_shard(merged[hop], hop, 0) for hop in range(shards)]
    ahead_home = [to_shard(merged[shards + hop], hop, 1) for hop in range(shards)]
    return pl.pallas_call(
        functools.partial(unpack_kernel, shards, cols),
        out_shape=[shape((tok, model), BF16)] * 4,
        in_specs=[whole(SMEM)] + [whole(VMEM)] * (3 * shards),
        out_specs=[whole(VMEM)] * 4,
        compiler_params=params(32),
        name="unpack",
    )(pos, *rows_home, *sums_home, *ahead_home)


def solution(mesh):
    sharded = P(("tm", "tile"), None)
    return jax.shard_map(
        per_device,
        mesh=mesh,
        in_specs=(sharded,) * 4 + (P(),) * 4,
        out_specs=(sharded,) * 4,
        check_vma=False,
    )
```

```python
import functools
import math

import jax
import jax.numpy as jnp
from jax import lax
from jax.experimental import pallas as pl
from jax.experimental.pallas import tpu as pltpu
from jax.sharding import PartitionSpec as P

VMEM = pltpu.VMEM
SMEM = pltpu.SMEM
BF16 = jnp.bfloat16
F32 = jnp.float32
NT = (((1,), (1,)), ((), ()))
LOG2E = 1.4426950408889634


def params(mib):
    return pltpu.CompilerParams(vmem_limit_bytes=mib * 1024 * 1024)


def whole(space):
    return pl.BlockSpec(memory_space=space)


def shard_count(heads, groups):
    count = 1
    while heads % (2 * count) == 0 and groups % (2 * count) == 0:
        count *= 2
    return count


def pack_kernel(shards, width, pos_ref, q_ref, g_ref, k_ref, v_ref, *outs):
    shard = pos_ref[0]
    for hop in range(shards):
        lane = pl.multiple_of((shard ^ hop) * width, 128)
        full, pair = outs[hop], outs[shards + hop]
        full[0] = q_ref[:, pl.ds(lane, width)]
        full[1] = g_ref[:, pl.ds(lane, width)]
        k = k_ref[:, pl.ds(lane, width)]
        v = v_ref[:, pl.ds(lane, width)]
        full[2] = k
        full[3] = v
        pair[0] = k
        pair[1] = v


def attention_kernel(shards, replicas, tiles, own_heads, batch, inv_root, *refs):
    slots = shards * replicas
    pos_ref, span_ref, live_ref, bias_ref = refs[:4]
    full = refs[4 : 4 + slots]
    ahead = refs[4 + slots : 4 + 2 * slots]
    outs = refs[4 + 2 * slots : 4 + 2 * slots + shards + replicas]
    rows_out, sums_out = outs[:shards], outs[shards:]
    kv, kt, vt, acc, score, dprob, both, ot, dqt = refs[4 + 2 * slots + shards + replicas :]
    tok, width = kv.shape[2] // 2, kv.shape[3] // 2
    shard, replica, tile = pos_ref[0], pos_ref[1], pos_ref[2]
    first = shard * own_heads + pl.program_id(0) * batch
    heads = range(batch)
    scale = inv_root * LOG2E

    def group_of(turn, hop):
        return (shard ^ hop) * replicas + lax.rem(replica + turn, replicas)

    def lanes(h):
        return pl.ds(h * width, width)

    for turn in range(replicas):
        for hop in range(shards):
            slot = turn * shards + hop
            span = span_ref[group_of(turn, hop)]
            for h in heads:
                for plane, (ref, at) in enumerate(((full[slot], 2), (ahead[slot], 0))):
                    part = pl.ds(plane * tok, tok)
                    k, v = ref[at, :, lanes(h)], ref[at + 1, :, lanes(h)]
                    kv[h, span, part, :width] = k
                    kv[h, span, part, width:] = v
                    kt[h, span, :, part] = k.T
                    vt[h, span, :, part] = v.T
    acc[...] = jnp.zeros_like(acc)
    both[...] = jnp.zeros_like(both)

    def fold(op, x):
        return op(x.reshape(x.shape[0] // 8, 8, x.shape[1]), axis=0)

    def query_tile(hop, count, rows):
        for h in heads:
            both[h, :tok, :width] = full[hop][0, :, lanes(h)]
            both[h, tok:, width:] = full[hop][1, :, lanes(h)]
        ot[...] = jnp.zeros_like(ot)
        dqt[...] = jnp.zeros_like(dqt)

        def score_step(i, peaks):
            new = []
            for h in heads:
                sd = lax.dot_general(kv[h, i, :rows, :], both[h], NT, preferred_element_type=F32)
                s = sd[:, :tok] * scale + bias_ref[i, first + h] * LOG2E
                score[h, i, :rows, :] = s
                dprob[h, i, :rows, :] = sd[:, tok:]
                new.append(jnp.maximum(peaks[h], fold(jnp.max, s)))
            return tuple(new)

        peaks = lax.fori_loop(
            0, count, score_step, tuple(jnp.full((8, tok), -3e38, F32) for _ in heads)
        )
        peaks = [jnp.max(x, axis=0, keepdims=True) for x in peaks]

        def total_step(i, carry):
            new = []
            for h in heads:
                e = jnp.exp2(score[h, i, :rows, :] - peaks[h])
                new.append(carry[2 * h] + fold(jnp.sum, e))
                new.append(carry[2 * h + 1] + fold(jnp.sum, e * dprob[h, i, :rows, :]))
            return tuple(new)

        totals = lax.fori_loop(
            0, count, total_step, tuple(jnp.zeros((8, tok), F32) for _ in range(2 * batch))
        )
        totals = [jnp.sum(x, axis=0, keepdims=True) for x in totals]
        log_total = [peaks[h] + jnp.log2(totals[2 * h]) for h in heads]
        delta = [totals[2 * h + 1] / totals[2 * h] for h in heads]

        def grad_step(i, carry):
            for h in heads:
                w = jnp.exp2(score[h, i, :rows, :] - log_total[h])
                ds = (w * (dprob[h, i, :rows, :] - delta[h])).astype(BF16)
                w = w.astype(BF16)
                acc[h, i, :rows, :] += jnp.dot(
                    jnp.concatenate([ds, w], axis=1), both[h], preferred_element_type=F32
                )
                ot[h] += jnp.dot(vt[h, i, :, :rows], w, preferred_element_type=F32)
                dqt[h] += jnp.dot(kt[h, i, :, :rows], ds, preferred_element_type=F32)
            return carry

        lax.fori_loop(0, count, grad_step, 0)
        for h in heads:
            rows_out[hop][0, :, lanes(h)] = ot[h].astype(BF16).T
            rows_out[hop][1, :, lanes(h)] = (dqt[h] * inv_root).astype(BF16).T

    for hop in range(shards):
        group = group_of(0, hop)
        count = span_ref[group] + 1
        live = live_ref[group * tiles + tile]

        @pl.when(live == 1)
        def _():
            query_tile(hop, count, 2 * tok)

        @pl.when(live != 1)
        def _():
            query_tile(hop, count, tok)

    for turn in range(replicas):
        for hop in range(shards):
            span = span_ref[group_of(turn, hop)]
            for h in heads:
                for plane in range(2):
                    part = pl.ds(plane * tok, tok)
                    sums_out[turn][hop, 2 * plane, :, lanes(h)] = (
                        acc[h, span, part, :width] * inv_root
                    ).astype(BF16)
                    sums_out[turn][hop, 2 * plane + 1, :, lanes(h)] = acc[
                        h, span, part, width:
                    ].astype(BF16)


def merge_kernel(shards, replicas, *refs):
    parts, outs = refs[:replicas], refs[replicas:]
    for hop in range(shards):
        for which in range(4):
            total = parts[0][hop, which].astype(F32)
            for part in parts[1:]:
                total = total + part[hop, which].astype(F32)
            outs[hop if which < 2 else shards + hop][which % 2] = total.astype(BF16)


def unpack_kernel(shards, width, pos_ref, *refs):
    rows, sums, ahead = refs[:shards], refs[shards : 2 * shards], refs[2 * shards : 3 * shards]
    out_ref, dq_ref, dk_ref, dv_ref = refs[3 * shards :]
    shard = pos_ref[0]
    for hop in range(shards):
        lanes = pl.ds(pl.multiple_of((shard ^ hop) * width, 128), width)
        out_ref[:, lanes] = rows[hop][0]
        dq_ref[:, lanes] = rows[hop][1]
        dk_ref[:, lanes] = (sums[hop][0].astype(F32) + ahead[hop][0].astype(F32)).astype(BF16)
        dv_ref[:, lanes] = (sums[hop][1].astype(F32) + ahead[hop][1].astype(F32)).astype(BF16)


def attend(sizes, pos, span_of_group, next_live, bias, full, ahead):
    shards, replicas, tiles, own_heads, width, tok = sizes
    groups = shards * replicas
    batch = own_heads if groups <= 8 else 1
    cols, step = own_heads * width, batch * width
    shape = jax.ShapeDtypeStruct

    def head_block(count):
        return pl.BlockSpec((count, tok, step), lambda h: (0, 0, h))

    stacked = pl.BlockSpec((shards, 4, tok, step), lambda h: (0, 0, 0, h))
    return pl.pallas_call(
        functools.partial(
            attention_kernel, shards, replicas, tiles, own_heads, batch, 1.0 / math.sqrt(width)
        ),
        grid=(own_heads // batch,),
        out_shape=[shape((2, tok, cols), BF16)] * shards
        + [shape((shards, 4, tok, cols), BF16)] * replicas,
        in_specs=[whole(SMEM)] * 4 + [head_block(4)] * groups + [head_block(2)] * groups,
        out_specs=[head_block(2)] * shards + [stacked] * replicas,
        scratch_shapes=[
            VMEM((batch, groups, 2 * tok, 2 * width), BF16),
            VMEM((batch, groups, width, 2 * tok), BF16),
            VMEM((batch, groups, width, 2 * tok), BF16),
            VMEM((batch, groups, 2 * tok, 2 * width), F32),
            VMEM((batch, groups, 2 * tok, tok), F32),
            VMEM((batch, groups, 2 * tok, tok), F32),
            VMEM((batch, 2 * tok, 2 * width), BF16),
            VMEM((batch, width, tok), F32),
            VMEM((batch, width, tok), F32),
        ],
        compiler_params=params(48),
        name="attention",
    )(pos, span_of_group, next_live, bias, *full, *ahead)


def per_device(queries, keys, values, grad_out, span_of_group, noise_level, next_live, level_bias):
    tok, model = queries.shape
    heads = level_bias.shape[1]
    width = model // heads
    groups = lax.axis_size("tm")
    tiles = lax.axis_size("tile")
    shards = shard_count(heads, groups)
    replicas = groups // shards
    own_heads = heads // shards
    cols = own_heads * width
    inv_root = 1.0 / math.sqrt(width)
    me = lax.axis_index("tm")
    shard, replica = me // replicas, me % replicas
    pos = jnp.stack([shard, replica, lax.axis_index("tile")]).astype(jnp.int32)
    shape = jax.ShapeDtypeStruct

    def to_shard(x, hop, lift):
        if hop == 0 and lift == 0:
            return x
        pairs = []
        for t in range(groups):
            goal = ((t // replicas) ^ hop) * replicas + t % replicas
            for s in range(tiles):
                pairs.append((t * tiles + s, goal * tiles + (s + lift) % tiles))
        return lax.ppermute(x, ("tm", "tile"), pairs)

    def to_replica(x, turn):
        pairs = [(t, t // replicas * replicas + (t - turn) % replicas) for t in range(groups)]
        return lax.ppermute(x, "tm", pairs)

    packed = pl.pallas_call(
        functools.partial(pack_kernel, shards, cols),
        out_shape=[shape((4, tok, cols), BF16)] * shards + [shape((2, tok, cols), BF16)] * shards,
        in_specs=[whole(SMEM)] + [whole(VMEM)] * 4,
        out_specs=[whole(VMEM)] * (2 * shards),
        compiler_params=params(32),
        name="pack",
    )(pos, queries, grad_out, keys, values)
    full = [to_shard(packed[hop], hop, 0) for hop in range(shards)]
    ahead = [to_shard(packed[shards + hop], hop, -1) for hop in range(shards)]
    full_all, ahead_all = list(full), list(ahead)
    for turn in range(1, replicas):
        full_all += [to_replica(x, turn) for x in full]
        ahead_all += [to_replica(x, turn) for x in ahead]
    bias = level_bias.at[noise_level].get(mode="promise_in_bounds")

    results = attend(
        (shards, replicas, tiles, own_heads, width, tok),
        pos, span_of_group, next_live, bias, full_all, ahead_all,
    )
    rows, sums = results[:shards], results[shards:]
    rows_home = [to_shard(rows[hop], hop, 0) for hop in range(shards)]
    parts = [sums[0]]
    for turn in range(1, replicas):
        parts.append(to_replica(sums[turn], replicas - turn))
    merged = pl.pallas_call(
        functools.partial(merge_kernel, shards, replicas),
        out_shape=[shape((2, tok, cols), BF16)] * (2 * shards),
        in_specs=[whole(VMEM)] * replicas,
        out_specs=[whole(VMEM)] * (2 * shards),
        compiler_params=params(48),
        name="merge",
    )(*parts)
    sums_home = [to_shard(merged[hop], hop, 0) for hop in range(shards)]
    ahead_home = [to_shard(merged[shards + hop], hop, 1) for hop in range(shards)]
    return pl.pallas_call(
        functools.partial(unpack_kernel, shards, cols),
        out_shape=[shape((tok, model), BF16)] * 4,
        in_specs=[whole(SMEM)] + [whole(VMEM)] * (3 * shards),
        out_specs=[whole(VMEM)] * 4,
        compiler_params=params(32),
        name="unpack",
    )(pos, *rows_home, *sums_home, *ahead_home)


def solution(mesh):
    sharded = P(("tm", "tile"), None)
    return jax.shard_map(
        per_device,
        mesh=mesh,
        in_specs=(sharded,) * 4 + (P(),) * 4,
        out_specs=(sharded,) * 4,
        check_vma=False,
    )
```

```python
import functools
import math

import jax
import jax.numpy as jnp
from jax import lax
from jax.experimental import pallas as pl
from jax.experimental.pallas import tpu as pltpu
from jax.sharding import PartitionSpec as P

VMEM = pltpu.VMEM
SMEM = pltpu.SMEM
BF16 = jnp.bfloat16
F32 = jnp.float32
NT = (((1,), (1,)), ((), ()))
LOG2E = 1.4426950408889634


def params(mib):
    return pltpu.CompilerParams(vmem_limit_bytes=mib * 1024 * 1024)


def whole(space):
    return pl.BlockSpec(memory_space=space)


def shard_count(heads, groups):
    count = 1
    while heads % (2 * count) == 0 and groups % (2 * count) == 0:
        count *= 2
    return count


def pack_kernel(shards, width, pos_ref, *refs):
    sources, outs, held, sems = refs[:4], refs[4:-2], refs[-2], refs[-1]
    shard = pos_ref[0]
    half = held.shape[1] // 2
    copies = []
    for i, src in enumerate(sources):
        for j in range(2):
            rows = pl.ds(j * half, half)
            copy = pltpu.make_async_copy(src.at[rows], held.at[i, rows], sems.at[i, j])
            copy.start()
            copies.append(copy)
    for i in (2, 3, 0, 1):
        copies[2 * i].wait()
        copies[2 * i + 1].wait()
        for hop in range(shards):
            part = held[i, :, pl.ds(pl.multiple_of((shard ^ hop) * width, 128), width)]
            outs[hop][i] = part
            if i >= 2:
                outs[shards + hop][i - 2] = part


def attention_kernel(shards, replicas, tiles, own_heads, batch, inv_root, *refs):
    slots = shards * replicas
    pos_ref, span_ref, live_ref, level_ref, table_ref = refs[:5]
    full, ahead = refs[5 : 5 + slots], refs[5 + slots : 5 + 2 * slots]
    outs = refs[5 + 2 * slots : 5 + 2 * slots + shards + replicas]
    rows_out, sums_out = outs[:shards], outs[shards:]
    kv, kt, vt, acc, score, dprob, both, ot, dqt, bias = refs[5 + 2 * slots + shards + replicas :]
    tok, width = kv.shape[2] // 2, kv.shape[3] // 2
    shard, replica, tile = pos_ref[0], pos_ref[1], pos_ref[2]
    first = shard * own_heads + (0 if batch == own_heads else pl.program_id(0) * batch)
    heads = range(batch)
    scale = inv_root * LOG2E

    def group_of(turn, hop):
        return (shard ^ hop) * replicas + lax.rem(replica + turn, replicas)

    def lanes(h):
        return pl.ds(h * width, width)

    for turn in range(replicas):
        for hop in range(shards):
            slot = turn * shards + hop
            span = span_ref[group_of(turn, hop)]
            for h in heads:
                for plane, (ref, at) in enumerate(((full[slot], 2), (ahead[slot], 0))):
                    part = pl.ds(plane * tok, tok)
                    k, v = ref[at, :, lanes(h)], ref[at + 1, :, lanes(h)]
                    kv[h, span, part, :width] = k
                    kv[h, span, part, width:] = v
                    kt[h, span, :, part] = k.T
                    vt[h, span, :, part] = v.T
    table = table_ref[...]
    level_ids = lax.broadcasted_iota(jnp.int32, table.shape, 1)
    for span in range(slots):
        column = jnp.sum(
            jnp.where(level_ids == level_ref[span], table, 0.0), axis=1, keepdims=True
        )
        bias[span] = jnp.broadcast_to(column * LOG2E, bias.shape[1:])
    acc[...] = jnp.zeros_like(acc)
    both[...] = jnp.zeros_like(both)

    def fold(op, x):
        return op(x.reshape(x.shape[0] // 8, 8, x.shape[1]), axis=0)

    def query_tile(hop, count, rows):
        for h in heads:
            both[h, :tok, :width] = full[hop][0, :, lanes(h)]
            both[h, tok:, width:] = full[hop][1, :, lanes(h)]
        ot[...] = jnp.zeros_like(ot)
        dqt[...] = jnp.zeros_like(dqt)

        def score_step(i, peaks):
            new = []
            for h in heads:
                sd = lax.dot_general(kv[h, i, :rows, :], both[h], NT, preferred_element_type=F32)
                s = sd[:, :tok] * scale + bias[i, pl.ds(first + h, 1), :]
                score[h, i, :rows, :] = s
                dprob[h, i, :rows, :] = sd[:, tok:]
                new.append(jnp.maximum(peaks[h], fold(jnp.max, s)))
            return tuple(new)

        peaks = lax.fori_loop(
            0, count, score_step, tuple(jnp.full((8, tok), -3e38, F32) for _ in heads)
        )
        peaks = [jnp.max(x, axis=0, keepdims=True) for x in peaks]

        def total_step(i, carry):
            new = []
            for h in heads:
                e = jnp.exp2(score[h, i, :rows, :] - peaks[h])
                new.append(carry[2 * h] + fold(jnp.sum, e))
                new.append(carry[2 * h + 1] + fold(jnp.sum, e * dprob[h, i, :rows, :]))
            return tuple(new)

        totals = lax.fori_loop(
            0, count, total_step, tuple(jnp.zeros((8, tok), F32) for _ in range(2 * batch))
        )
        totals = [jnp.sum(x, axis=0, keepdims=True) for x in totals]
        log_total = [peaks[h] + jnp.log2(totals[2 * h]) for h in heads]
        delta = [totals[2 * h + 1] / totals[2 * h] for h in heads]

        def grad_step(i, carry):
            for h in heads:
                w = jnp.exp2(score[h, i, :rows, :] - log_total[h])
                ds = (w * (dprob[h, i, :rows, :] - delta[h])).astype(BF16)
                w = w.astype(BF16)
                acc[h, i, :rows, :] += jnp.dot(
                    jnp.concatenate([ds, w], axis=1), both[h], preferred_element_type=F32
                )
                ot[h] += jnp.dot(vt[h, i, :, :rows], w, preferred_element_type=F32)
                dqt[h] += jnp.dot(kt[h, i, :, :rows], ds, preferred_element_type=F32)
            return carry

        lax.fori_loop(0, count, grad_step, 0)
        for h in heads:
            rows_out[hop][0, :, lanes(h)] = ot[h].astype(BF16).T
            rows_out[hop][1, :, lanes(h)] = (dqt[h] * inv_root).astype(BF16).T

    for hop in range(shards):
        group = group_of(0, hop)
        count = span_ref[group] + 1
        live = live_ref[group * tiles + tile]

        @pl.when(live == 1)
        def _():
            query_tile(hop, count, 2 * tok)

        @pl.when(live != 1)
        def _():
            query_tile(hop, count, tok)

    for turn in range(replicas):
        for hop in range(shards):
            span = span_ref[group_of(turn, hop)]
            for h in heads:
                for plane in range(2):
                    part = pl.ds(plane * tok, tok)
                    sums_out[turn][hop, 2 * plane, :, lanes(h)] = (
                        acc[h, span, part, :width] * inv_root
                    ).astype(BF16)
                    sums_out[turn][hop, 2 * plane + 1, :, lanes(h)] = acc[
                        h, span, part, width:
                    ].astype(BF16)


def merge_kernel(shards, replicas, *refs):
    parts, outs = refs[:replicas], refs[replicas:]
    for hop in range(shards):
        for which in range(4):
            total = parts[0][hop, which].astype(F32)
            for part in parts[1:]:
                total = total + part[hop, which].astype(F32)
            outs[hop if which < 2 else shards + hop][which % 2] = total.astype(BF16)


def unpack_kernel(shards, width, pos_ref, *refs):
    rows, sums, ahead = refs[:shards], refs[shards : 2 * shards], refs[2 * shards : 3 * shards]
    out_ref, dq_ref, dk_ref, dv_ref = refs[3 * shards :]
    shard = pos_ref[0]
    for hop in range(shards):
        lanes = pl.ds(pl.multiple_of((shard ^ hop) * width, 128), width)
        out_ref[:, lanes] = rows[hop][0]
        dq_ref[:, lanes] = rows[hop][1]
        dk_ref[:, lanes] = (sums[hop][0].astype(F32) + ahead[hop][0].astype(F32)).astype(BF16)
        dv_ref[:, lanes] = (sums[hop][1].astype(F32) + ahead[hop][1].astype(F32)).astype(BF16)


def attend(sizes, pos, span_of_group, next_live, noise_level, bias_table, full, ahead):
    shards, replicas, tiles, own_heads, width, tok = sizes
    groups = shards * replicas
    batch = own_heads if groups <= 8 else 1
    cols, step = own_heads * width, batch * width
    shape = jax.ShapeDtypeStruct

    if batch == own_heads:
        grid = ()
        narrow = wide = stacked = whole(VMEM)
    else:
        grid = (own_heads // batch,)
        narrow = pl.BlockSpec((2, tok, step), lambda h: (0, 0, h))
        wide = pl.BlockSpec((4, tok, step), lambda h: (0, 0, h))
        stacked = pl.BlockSpec((shards, 4, tok, step), lambda h: (0, 0, 0, h))
    return pl.pallas_call(
        functools.partial(
            attention_kernel, shards, replicas, tiles, own_heads, batch, 1.0 / math.sqrt(width)
        ),
        grid=grid,
        out_shape=[shape((2, tok, cols), BF16)] * shards
        + [shape((shards, 4, tok, cols), BF16)] * replicas,
        in_specs=[whole(SMEM)] * 4 + [whole(VMEM)] + [wide] * groups + [narrow] * groups,
        out_specs=[narrow] * shards + [stacked] * replicas,
        scratch_shapes=[
            VMEM((batch, groups, 2 * tok, 2 * width), BF16),
            VMEM((batch, groups, width, 2 * tok), BF16),
            VMEM((batch, groups, width, 2 * tok), BF16),
            VMEM((batch, groups, 2 * tok, 2 * width), F32),
            VMEM((batch, groups, 2 * tok, tok), F32),
            VMEM((batch, groups, 2 * tok, tok), F32),
            VMEM((batch, 2 * tok, 2 * width), BF16),
            VMEM((batch, width, tok), F32),
            VMEM((batch, width, tok), F32),
            VMEM((groups, bias_table.shape[0], tok), F32),
        ],
        compiler_params=params(30 if batch == own_heads else 48),
        name="attention",
    )(pos, span_of_group, next_live, noise_level, bias_table, *full, *ahead)


def per_device(queries, keys, values, grad_out, span_of_group, noise_level, next_live, level_bias):
    tok, model = queries.shape
    heads = level_bias.shape[1]
    width = model // heads
    groups = lax.axis_size("tm")
    tiles = lax.axis_size("tile")
    shards = shard_count(heads, groups)
    replicas = groups // shards
    own_heads = heads // shards
    cols = own_heads * width
    inv_root = 1.0 / math.sqrt(width)
    me = lax.axis_index("tm")
    shard, replica = me // replicas, me % replicas
    pos = jnp.stack([shard, replica, lax.axis_index("tile")]).astype(jnp.int32)
    shape = jax.ShapeDtypeStruct

    def to_shard(x, hop, lift):
        if hop == 0 and lift == 0:
            return x
        pairs = []
        for t in range(groups):
            goal = ((t // replicas) ^ hop) * replicas + t % replicas
            for s in range(tiles):
                pairs.append((t * tiles + s, goal * tiles + (s + lift) % tiles))
        return lax.ppermute(x, ("tm", "tile"), pairs)

    def to_replica(x, turn):
        pairs = [(t, t // replicas * replicas + (t - turn) % replicas) for t in range(groups)]
        return lax.ppermute(x, "tm", pairs)

    packed = pl.pallas_call(
        functools.partial(pack_kernel, shards, cols),
        out_shape=[shape((4, tok, cols), BF16)] * shards + [shape((2, tok, cols), BF16)] * shards,
        in_specs=[whole(SMEM)] + [whole(pltpu.HBM)] * 4,
        out_specs=[whole(VMEM)] * (2 * shards),
        scratch_shapes=[VMEM((4, tok, model), BF16), pltpu.SemaphoreType.DMA((4, 2))],
        compiler_params=params(8),
        name="pack",
    )(pos, *(pltpu.with_memory_space_constraint(x, pltpu.HBM) for x in (queries, grad_out, keys, values)))
    full = [to_shard(packed[hop], hop, 0) for hop in range(shards)]
    ahead = [to_shard(packed[shards + hop], hop, -1) for hop in range(shards)]
    full_all, ahead_all = list(full), list(ahead)
    for turn in range(1, replicas):
        full_all += [to_replica(x, turn) for x in full]
        ahead_all += [to_replica(x, turn) for x in ahead]

    results = attend(
        (shards, replicas, tiles, own_heads, width, tok),
        pos, span_of_group, next_live, noise_level, level_bias.T, full_all, ahead_all,
    )
    rows, sums = results[:shards], results[shards:]
    rows_home = [to_shard(rows[hop], hop, 0) for hop in range(shards)]
    parts = [sums[0]]
    for turn in range(1, replicas):
        parts.append(to_replica(sums[turn], replicas - turn))
    merged = pl.pallas_call(
        functools.partial(merge_kernel, shards, replicas),
        out_shape=[shape((2, tok, cols), BF16)] * (2 * shards),
        in_specs=[whole(VMEM)] * replicas,
        out_specs=[whole(VMEM)] * (2 * shards),
        compiler_params=params(8),
        name="merge",
    )(*parts)
    sums_home = [to_shard(merged[hop], hop, 0) for hop in range(shards)]
    ahead_home = [to_shard(merged[shards + hop], hop, 1) for hop in range(shards)]
    return pl.pallas_call(
        functools.partial(unpack_kernel, shards, cols),
        out_shape=[shape((tok, model), BF16)] * 4,
        in_specs=[whole(SMEM)] + [whole(VMEM)] * (3 * shards),
        out_specs=[whole(VMEM)] * 4,
        compiler_params=params(8),
        name="unpack",
    )(pos, *rows_home, *sums_home, *ahead_home)


def solution(mesh):
    sharded = P(("tm", "tile"), None)
    return jax.shard_map(
        per_device,
        mesh=mesh,
        in_specs=(sharded,) * 4 + (P(),) * 4,
        out_specs=(sharded,) * 4,
        check_vma=False,
    )
```

```python
import functools
import math

import jax
import jax.numpy as jnp
from jax import lax
from jax.experimental import pallas as pl
from jax.experimental.pallas import tpu as pltpu
from jax.sharding import PartitionSpec as P

VMEM = pltpu.VMEM
SMEM = pltpu.SMEM
BF16 = jnp.bfloat16
F32 = jnp.float32
NT = (((1,), (1,)), ((), ()))
LOG2E = 1.4426950408889634
DEAD = -1e30


def params(mib):
    return pltpu.CompilerParams(vmem_limit_bytes=mib * 1024 * 1024)


def whole(space):
    return pl.BlockSpec(memory_space=space)


def shard_count(heads, groups):
    count = 1
    while heads % (2 * count) == 0 and groups % (2 * count) == 0:
        count *= 2
    return count


def fold(op, x):
    return op(x.reshape(x.shape[0] // 8, 8, x.shape[1]), axis=0)


def pack_kernel(z, pos_ref, *refs):
    sources, table_ref, refs = refs[:4], refs[4], refs[5:]
    outs, (pair, table, held, sems, table_sem) = refs[: z.shards], refs[z.shards :]
    half, cols = z.tok // 2, z.own_heads * z.width
    places = [pair.at[0], pair.at[1], held.at[0], held.at[1]]
    copies = []
    for i, src in enumerate(sources):
        for j in range(2):
            rows = pl.ds(j * half, half)
            copy = pltpu.make_async_copy(src.at[rows], places[i].at[rows], sems.at[i, j])
            copy.start()
            copies.append(copy)
    table_copy = pltpu.make_async_copy(table_ref, table, table_sem)
    table_copy.start()
    for i in range(4):
        copies[2 * i].wait()
        copies[2 * i + 1].wait()
        for hop in range(z.shards):
            lanes = pl.ds(pl.multiple_of((pos_ref[0] ^ hop) * cols, 128), cols)
            outs[hop][i] = places[i][:, lanes]
    table_copy.wait()


def pack(z, pos, arrays, table):
    cols = z.own_heads * z.width
    sources = [pltpu.with_memory_space_constraint(x, pltpu.HBM) for x in (*arrays, table)]
    shape = jax.ShapeDtypeStruct
    results = pl.pallas_call(
        functools.partial(pack_kernel, z),
        out_shape=[shape((4, z.tok, cols), BF16)] * z.shards
        + [shape((2, z.tok, cols * z.shards), BF16), shape(table.shape, F32)],
        in_specs=[whole(SMEM)] + [whole(pltpu.HBM)] * 5,
        out_specs=[whole(VMEM)] * (z.shards + 2),
        scratch_shapes=[
            VMEM((2, z.tok, cols * z.shards), BF16),
            pltpu.SemaphoreType.DMA((4, 2)),
            pltpu.SemaphoreType.DMA,
        ],
        compiler_params=params(8),
        name="pack",
    )(pos, *sources)
    return results[:-2], results[-2], results[-1]


def cut_kernel(z, pos_ref, both_ref, *outs):
    cols = z.own_heads * z.width
    for hop in range(z.shards):
        lanes = pl.ds(pl.multiple_of((pos_ref[0] ^ hop) * cols, 128), cols)
        for i in range(2):
            outs[hop][i] = both_ref[i, :, lanes]


def cut(z, pos, both):
    shape = jax.ShapeDtypeStruct((2, z.tok, z.own_heads * z.width), BF16)
    return pl.pallas_call(
        functools.partial(cut_kernel, z),
        out_shape=[shape] * z.shards,
        in_specs=[whole(SMEM), whole(VMEM)],
        out_specs=[whole(VMEM)] * z.shards,
        compiler_params=params(8),
        name="cut",
    )(pos, both)


def after_kernel(*refs):
    pass


def after(x, *others):
    return pl.pallas_call(
        after_kernel,
        out_shape=jax.ShapeDtypeStruct(x.shape, x.dtype),
        in_specs=[whole(pl.ANY)] * (1 + len(others)),
        out_specs=whole(pl.ANY),
        input_output_aliases={0: 0},
        compiler_params=params(1),
        name="after",
    )(x, *others)


class Sizes:
    def __init__(self, shards, replicas, tiles, own_heads, width, tok):
        self.shards, self.replicas, self.tiles = shards, replicas, tiles
        self.own_heads, self.width, self.tok = own_heads, width, tok
        self.groups = shards * replicas
        self.batch = own_heads if self.groups <= 8 else 1
        self.inv_root = 1.0 / math.sqrt(width)

    def group_of(self, meta_ref, turn, hop):
        return (meta_ref[0] ^ hop) * self.replicas + lax.rem(meta_ref[1] + turn, self.replicas)

    def span(self, meta_ref, turn, hop):
        return meta_ref[3 + self.group_of(meta_ref, turn, hop)]

    def level(self, meta_ref, span):
        return meta_ref[3 + self.groups + span]

    def live(self, meta_ref, hop):
        tile = self.group_of(meta_ref, 0, hop) * self.tiles + meta_ref[2]
        return meta_ref[3 + 2 * self.groups + tile]

    def slots(self, meta_ref):
        for turn in range(self.replicas):
            for hop in range(self.shards):
                yield turn, hop, self.span(meta_ref, turn, hop)

    def lanes(self, h):
        return pl.ds(h * self.width, self.width)

    def first_head(self, meta_ref):
        base = 0 if self.batch == self.own_heads else pl.program_id(0) * self.batch
        return meta_ref[0] * self.own_heads + base

    def steps(self, count):
        return lax.div(count + 1, 2)

    def call(self, kernel, name, limit, operands, outs, scratch):
        split = self.batch != self.own_heads

        def spec(shape, kind):
            if kind == "scalar":
                return whole(SMEM)
            if not split:
                return whole(VMEM)
            block, axis = list(shape), {"heads": 0, "lanes": len(shape) - 1}.get(kind)
            if axis is None:
                return pl.BlockSpec(tuple(block), lambda h: (0,) * len(block))
            block[axis] = block[axis] // self.own_heads * self.batch
            return pl.BlockSpec(
                tuple(block), lambda h: tuple(h if d == axis else 0 for d in range(len(block)))
            )

        return pl.pallas_call(
            functools.partial(kernel, self),
            grid=(self.own_heads // self.batch,) if split else (),
            in_specs=[spec(x.shape, kind) for x, kind in operands],
            out_specs=[spec(x.shape, kind) for x, kind in outs],
            out_shape=[x for x, kind in outs],
            scratch_shapes=scratch,
            compiler_params=params(limit),
            name=name,
        )(*(x for x, kind in operands))


def order_tiles(z, meta_ref, tiles, kv, kt, vt):
    for turn, hop, span in z.slots(meta_ref):
        ref = tiles[turn * z.shards + hop]
        rows = pl.ds(pl.multiple_of(span * z.tok, z.tok), z.tok)
        half = pl.ds(pl.multiple_of(lax.rem(span, 2) * z.tok, z.tok), z.tok)
        for h in range(z.batch):
            k, v = ref[0, :, z.lanes(h)], ref[1, :, z.lanes(h)]
            kv[h, rows, : z.width] = k
            kv[h, rows, z.width :] = v
            kt[h, lax.div(span, 2), :, half] = k.T
            vt[h, lax.div(span, 2), :, half] = v.T


def softmax_sums(z, first, count, bias, kv, both, score, dprob):
    heads, tok = range(z.batch), z.tok
    scale = z.inv_root * LOG2E

    def score_step(c, peaks):
        rows = pl.ds(pl.multiple_of(c * 2 * tok, 2 * tok), 2 * tok)
        new = []
        for h in heads:
            sd = lax.dot_general(kv[h, rows, :], both[h][...], NT, preferred_element_type=F32)
            peak = peaks[h]
            for j in range(2):
                part = slice(j * tok, (j + 1) * tok)
                span = 2 * c + j
                shift = bias[span, pl.ds(first + h, 1), :] + jnp.where(span < count, 0.0, DEAD)
                s = sd[part, :tok] * scale + shift
                score[h][c, part, :] = s
                peak = jnp.maximum(peak, fold(jnp.max, s))
            dprob[h][c] = sd[:, tok:]
            new.append(peak)
        return tuple(new)

    peaks = lax.fori_loop(
        0, z.steps(count), score_step, tuple(jnp.full((8, tok), -3e38, F32) for _ in heads)
    )
    peaks = [jnp.max(x, axis=0, keepdims=True) for x in peaks]

    def total_step(c, carry):
        new = []
        for h in heads:
            e = jnp.exp2(score[h][c] - peaks[h])
            new.append(carry[2 * h] + fold(jnp.sum, e))
            new.append(carry[2 * h + 1] + fold(jnp.sum, e * dprob[h][c]))
        return tuple(new)

    totals = lax.fori_loop(
        0, z.steps(count), total_step, tuple(jnp.zeros((8, tok), F32) for _ in range(2 * z.batch))
    )
    totals = [jnp.sum(x, axis=0, keepdims=True) for x in totals]
    return peaks, totals[::2], totals[1::2]


def gradients(z, count, log_total, delta, score, dprob, both, kt, vt, acc, ot, dqt):
    def grad_step(c, carry):
        rows = pl.ds(pl.multiple_of(c * 2 * z.tok, 2 * z.tok), 2 * z.tok)
        for h in range(z.batch):
            w = jnp.exp2(score[h][c] - log_total[h])
            ds = (w * (dprob[h][c] - delta[h])).astype(BF16)
            w = w.astype(BF16)
            acc[h, rows, :] += jnp.dot(
                jnp.concatenate([ds, w], axis=1), both[h][...], preferred_element_type=F32
            )
            ot[h][...] += jnp.dot(vt[h, c], w, preferred_element_type=F32)
            dqt[h][...] += jnp.dot(kt[h, c], ds, preferred_element_type=F32)
        return carry

    lax.fori_loop(0, z.steps(count), grad_step, 0)


def write_sums(z, meta_ref, acc, sums):
    for turn, hop, span in z.slots(meta_ref):
        goal = sums[turn * z.shards + hop]
        rows = pl.ds(pl.multiple_of(span * z.tok, z.tok), z.tok)
        for h in range(z.batch):
            goal[0, :, z.lanes(h)] = (acc[h, rows, : z.width] * z.inv_root).astype(BF16)
            goal[1, :, z.lanes(h)] = acc[h, rows, z.width :].astype(BF16)


def own_kernel(z, meta_ref, table_ref, *refs):
    full, refs = refs[: z.groups], refs[z.groups :]
    kt, vt, both, bias, score, dprob, stats, kv = refs
    first = z.first_head(meta_ref)
    order_tiles(z, meta_ref, full, kv, kt, vt)
    level_ids = lax.broadcasted_iota(jnp.int32, table_ref.shape, 1)
    for span in range(z.groups):
        column = jnp.sum(
            jnp.where(level_ids == z.level(meta_ref, span), table_ref[...], 0.0),
            axis=1,
            keepdims=True,
        )
        bias[span] = jnp.broadcast_to(column * LOG2E, bias.shape[1:])
    for hop in range(z.shards):
        for h in range(z.batch):
            for i in range(2):
                for j in range(2):
                    block = full[hop][2 + i, :, z.lanes(h)]
                    both[h, hop, pl.ds(i * z.tok, z.tok), z.lanes(j)] = (
                        block if i == j else jnp.zeros_like(block)
                    )
        count = z.span(meta_ref, 0, hop) + 1
        heads = range(z.batch)
        sums = softmax_sums(
            z,
            first,
            count,
            bias,
            kv,
            [both.at[h, hop] for h in heads],
            [score.at[h, hop] for h in heads],
            [dprob.at[h, hop] for h in heads],
        )
        for h in heads:
            for i in range(3):
                stats[h, hop, i : i + 1, :] = sums[i][h]


def ahead_kernel(z, meta_ref, bias, both, stats, *refs):
    tiles, refs = refs[: z.groups], refs[z.groups :]
    (final, ot, dqt), sums, refs = refs[:3], refs[3 : 3 + z.groups], refs[3 + z.groups :]
    kv, kt, vt, score, dprob, acc = refs
    first = z.first_head(meta_ref)
    heads = range(z.batch)
    order_tiles(z, meta_ref, tiles, kv, kt, vt)
    acc[...] = jnp.zeros_like(acc)
    ot[...] = jnp.zeros_like(ot)
    dqt[...] = jnp.zeros_like(dqt)
    for hop in range(z.shards):
        count = z.span(meta_ref, 0, hop) + 1
        live = z.live(meta_ref, hop)
        near = [[stats[h, hop, i : i + 1, :] for h in heads] for i in range(3)]

        @pl.when(live != 1)
        def _():
            for h in heads:
                final[h, hop, 0:1, :] = near[0][h] + jnp.log2(near[1][h])
                final[h, hop, 1:2, :] = near[2][h] / near[1][h]

        @pl.when(live == 1)
        def _():
            views = (
                [score.at[h] for h in heads],
                [dprob.at[h] for h in heads],
                [both.at[h, hop] for h in heads],
            )
            far = softmax_sums(z, first, count, bias, kv, views[2], views[0], views[1])
            log_total, delta = [], []
            for h in heads:
                peak = jnp.maximum(near[0][h], far[0][h])
                a, b = jnp.exp2(near[0][h] - peak), jnp.exp2(far[0][h] - peak)
                total = near[1][h] * a + far[1][h] * b
                log_total.append(peak + jnp.log2(total))
                delta.append((near[2][h] * a + far[2][h] * b) / total)
                final[h, hop, 0:1, :] = log_total[h]
                final[h, hop, 1:2, :] = delta[h]
            gradients(
                z,
                count,
                log_total,
                delta,
                *views,
                kt,
                vt,
                acc,
                [ot.at[h, hop] for h in heads],
                [dqt.at[h, hop] for h in heads],
            )

    write_sums(z, meta_ref, acc, sums)


def rows_kernel(z, meta_ref, kt, vt, both, score, dprob, final, ot_in, dqt_in, *refs):
    refs = refs[1:]
    rows_out, sums, refs = refs[: z.shards], refs[z.shards : z.shards + z.groups], refs[-3:]
    acc, ot, dqt = refs
    heads = range(z.batch)
    acc[...] = jnp.zeros_like(acc)
    for hop in range(z.shards):
        count = z.span(meta_ref, 0, hop) + 1
        for h in heads:
            ot[h] = ot_in[h, hop]
            dqt[h] = dqt_in[h, hop]
        gradients(
            z,
            count,
            [final[h, hop, 0:1, :] for h in heads],
            [final[h, hop, 1:2, :] for h in heads],
            [score.at[h, hop] for h in heads],
            [dprob.at[h, hop] for h in heads],
            [both.at[h, hop] for h in heads],
            kt,
            vt,
            acc,
            [ot.at[h] for h in heads],
            [dqt.at[h] for h in heads],
        )
        for h in heads:
            rows_out[hop][0, :, z.lanes(h)] = ot[h].astype(BF16).T
            rows_out[hop][1, :, z.lanes(h)] = (dqt[h] * z.inv_root).astype(BF16).T
    write_sums(z, meta_ref, acc, sums)


def add_up(terms, at=()):
    total = terms[0][at].astype(F32)
    for term in terms[1:]:
        total = total + term[at].astype(F32)
    return total.astype(BF16)


def join(lists):
    count = len(lists[0])

    def kernel(*refs):
        for i in range(len(lists)):
            for which in range(2):
                refs[-1][i, which] = add_up(refs[i * count : (i + 1) * count], which)

    operands = [x for parts in lists for x in parts]
    return pl.pallas_call(
        kernel,
        out_shape=jax.ShapeDtypeStruct((len(lists),) + operands[0].shape, BF16),
        in_specs=[whole(VMEM)] * len(operands),
        out_specs=whole(VMEM),
        compiler_params=params(8),
        name="join",
    )(*operands)


def merge(lists, joined, last):
    count = len(lists[0])

    def kernel(*refs):
        refs, outs = refs[: -1 - len(lists)], refs[-1 - len(lists) :]
        arrived, refs = refs[0], refs[1:]
        for which in range(2):
            for i in range(len(lists)):
                terms = list(refs[i * count : (i + 1) * count]) + [arrived.at[i]]
                outs[i][which] = add_up(terms, which)
            outs[-1][which] = add_up(refs[len(lists) * count :], which)

    operands = [joined] + [x for parts in lists for x in parts] + last
    return pl.pallas_call(
        kernel,
        out_shape=[jax.ShapeDtypeStruct(last[0].shape, BF16)] * (len(lists) + 1),
        in_specs=[whole(VMEM)] * len(operands),
        out_specs=[whole(VMEM)] * (len(lists) + 1),
        compiler_params=params(8),
        name="merge",
    )(*operands)


def unpack_kernel(shards, cols, pos_ref, *refs):
    parts, first, outs = refs[: shards - 1], refs[shards - 1 : -2], refs[-2:]
    for hop in range(shards):
        lanes = pl.ds(pl.multiple_of((pos_ref[0] ^ hop) * cols, 128), cols)
        for i in range(2):
            outs[i][:, lanes] = parts[hop - 1][i] if hop else add_up(first, i)


def unpack(pos, first, parts):
    tok, cols = parts[0].shape[1:]
    shards = len(parts) + 1
    return pl.pallas_call(
        functools.partial(unpack_kernel, shards, cols),
        out_shape=[jax.ShapeDtypeStruct((tok, cols * shards), BF16)] * 2,
        in_specs=[whole(SMEM)] + [whole(VMEM)] * (len(parts) + len(first)),
        out_specs=[whole(VMEM)] * 2,
        compiler_params=params(8),
        name="unpack",
    )(pos, *parts, *first)


def per_device(queries, keys, values, grad_out, span_of_group, noise_level, next_live, level_bias):
    tok, model = queries.shape
    heads = level_bias.shape[1]
    width = model // heads
    groups = lax.axis_size("tm")
    tiles = lax.axis_size("tile")
    shards = shard_count(heads, groups)
    replicas = groups // shards
    own = heads // shards
    cols = own * width
    z = Sizes(shards, replicas, tiles, own, width, tok)
    me = lax.axis_index("tm")
    pos = jnp.stack([me // replicas, me % replicas, lax.axis_index("tile")]).astype(jnp.int32)
    meta = jnp.concatenate([pos, span_of_group, noise_level, next_live])
    shape = jax.ShapeDtypeStruct

    def to_shard(x, hop, lift):
        if hop == 0 and lift == 0:
            return x
        pairs = []
        for t in range(groups):
            goal = ((t // replicas) ^ hop) * replicas + t % replicas
            for s in range(tiles):
                pairs.append((t * tiles + s, goal * tiles + (s + lift) % tiles))
        return lax.ppermute(x, ("tm", "tile"), pairs)

    def to_replica(x, turn):
        pairs = [(t, t // replicas * replicas + (t - turn) % replicas) for t in range(groups)]
        return lax.ppermute(x, "tm", pairs)

    def with_others(parts):
        return [
            [parts[hop]]
            + [
                to_replica(parts[turn * shards + hop], replicas - turn)
                for turn in range(1, replicas)
            ]
            for hop in hops
        ]

    def swapped(tiles):
        return [to_replica(x, turn) for turn in range(1, replicas) for x in tiles]

    hops = range(shards)
    packed, pair_raw, table = pack(z, pos, (keys, values, queries, grad_out), level_bias.T)
    full = [to_shard(packed[hop], hop, 0) for hop in hops]
    pair_far = to_shard(pair_raw, 0, -1)
    full += swapped(full)
    packed = cut(z, pos, pair_far)
    far = [to_shard(packed[hop], hop, 0) for hop in hops]

    scalars = [(meta, "scalar")]
    pair = shape((2, tok, cols), BF16)
    half = groups // 2
    square = shape((own, half, width, 2 * tok), BF16)
    block = shape((own, shards, half, 2 * tok, tok), F32)
    stat = shape((own, shards, 8, tok), F32)
    part = shape((own, shards, width, tok), F32)
    batch = z.batch
    kt, vt, both, bias, score, dprob, stats = z.call(
        own_kernel,
        "own",
        8 if batch == own else 48,
        scalars
        + [(table, "all")]
        + [(x, "lanes") for x in full],
        [
            (square, "heads"),
            (square, "heads"),
            (shape((own, shards, 2 * tok, 2 * width), BF16), "heads"),
            (shape((groups, heads, tok), F32), "all"),
            (block, "heads"),
            (block, "heads"),
            (stat, "heads"),
        ],
        [
            VMEM((batch, groups * tok, 2 * width), BF16),
        ],
    )
    far = [after(x, stats) for x in far]
    far += swapped(far)
    results = z.call(
        ahead_kernel,
        "ahead",
        16 if batch == own else 48,
        scalars
        + [(bias, "all"), (both, "heads"), (stats, "heads")]
        + [(x, "lanes") for x in far],
        [(stat, "heads"), (part, "heads"), (part, "heads")]
        + [(pair, "lanes")] * groups,
        [
            VMEM((batch, groups * tok, 2 * width), BF16),
            VMEM((batch, half, width, 2 * tok), BF16),
            VMEM((batch, half, width, 2 * tok), BF16),
            VMEM((batch, half, 2 * tok, tok), F32),
            VMEM((batch, half, 2 * tok, tok), F32),
            VMEM((batch, groups * tok, 2 * width), F32),
        ],
    )
    final, ot, dqt = results[:3]
    far_parts = with_others(results[3:])
    far_sums = join(far_parts[1:])
    far_home = to_shard(far_sums, 0, 1)
    results = z.call(
        rows_kernel,
        "rows",
        8 if batch == own else 48,
        scalars
        + [(x, "heads") for x in (kt, vt, both, score, dprob, final, ot, dqt)]
        + [(far_sums, "lanes")],
        [(pair, "lanes")] * (shards + groups),
        [
            VMEM((batch, groups * tok, 2 * width), F32),
            VMEM((batch, width, tok), F32),
            VMEM((batch, width, tok), F32),
        ],
    )
    rows_home = [to_shard(results[hop], hop, 0) for hop in hops]
    near_parts = with_others(results[shards:])
    *sums, far_last = merge(near_parts[1:], far_home, far_parts[0])
    sums_home = [to_shard(x, hop, 0) for hop, x in zip(hops[1:], sums)]
    last_home = to_shard(far_last, 0, 1)
    attended, grad_queries = unpack(pos, rows_home[:1], rows_home[1:])
    grad_keys, grad_values = unpack(pos, near_parts[0] + [last_home], sums_home)
    return attended, grad_queries, grad_keys, grad_values


def solution(mesh):
    sharded = P(("tm", "tile"), None)
    return jax.shard_map(
        per_device,
        mesh=mesh,
        in_specs=(sharded,) * 4 + (P(),) * 4,
        out_specs=(sharded,) * 4,
        check_vma=False,
    )
```

```python
import functools
import math

import jax
import jax.numpy as jnp
from jax import lax
from jax.experimental import pallas as pl
from jax.experimental.pallas import tpu as pltpu
from jax.sharding import PartitionSpec as P

VMEM = pltpu.VMEM
SMEM = pltpu.SMEM
BF16 = jnp.bfloat16
F32 = jnp.float32
NT = (((1,), (1,)), ((), ()))
LOG2E = 1.4426950408889634
DEAD = -1e30


def params(mib):
    return pltpu.CompilerParams(vmem_limit_bytes=mib * 1024 * 1024)


def whole(space):
    return pl.BlockSpec(memory_space=space)


def shard_count(heads, groups):
    count = 1
    while heads % (2 * count) == 0 and groups % (2 * count) == 0:
        count *= 2
    return count


def fold(op, x):
    return op(x.reshape(x.shape[0] // 8, 8, x.shape[1]), axis=0)


def pack_kernel(z, pos_ref, *refs):
    sources, refs = refs[:4], refs[4:]
    outs, (pair, early, held, sems) = refs[: z.shards], refs[z.shards :]
    half, cols = z.tok // 2, z.own_heads * z.width
    copies = []
    for i, src in enumerate(sources):
        for j in range(2):
            rows = pl.ds(j * half, half)
            copy = pltpu.make_async_copy(src.at[rows], held.at[i, rows], sems.at[i, j])
            copy.start()
            copies.append(copy)
    for i in range(4):
        copies[2 * i].wait()
        copies[2 * i + 1].wait()
        for hop in range(z.shards):
            lanes = pl.ds(pl.multiple_of((pos_ref[0] ^ hop) * cols, 128), cols)
            part = held[i, :, lanes]
            outs[hop][i] = part
            if hop == 0 and i < 2:
                pair[i] = part
            if hop == z.shards - 1 and i < 2:
                early[i] = part


def pack(z, pos, arrays):
    cols = z.own_heads * z.width
    sources = [pltpu.with_memory_space_constraint(x, pltpu.HBM) for x in arrays]
    shape = jax.ShapeDtypeStruct
    results = pl.pallas_call(
        functools.partial(pack_kernel, z),
        out_shape=[shape((4, z.tok, cols), BF16)] * z.shards
        + [shape((2, z.tok, cols), BF16)] * 2,
        in_specs=[whole(SMEM)] + [whole(pltpu.HBM)] * 4,
        out_specs=[whole(VMEM)] * (z.shards + 2),
        scratch_shapes=[
            VMEM((4, z.tok, cols * z.shards), BF16),
            pltpu.SemaphoreType.DMA((4, 2)),
        ],
        compiler_params=params(8),
        name="pack",
    )(pos, *sources)
    return results[:-2], results[-2], results[-1]


def bias_kernel(z, meta_ref, table_ref, after_ref, bias):
    level_ids = lax.broadcasted_iota(jnp.int32, table_ref.shape, 1)
    for span in range(z.groups):
        column = jnp.sum(
            jnp.where(level_ids == z.level(meta_ref, span), table_ref[...], 0.0),
            axis=1,
            keepdims=True,
        )
        bias[span] = jnp.broadcast_to(column * LOG2E, bias.shape[1:])


def bias_rows(z, meta, table, other):
    return pl.pallas_call(
        functools.partial(bias_kernel, z),
        out_shape=jax.ShapeDtypeStruct((z.groups, table.shape[0], z.tok), F32),
        in_specs=[whole(SMEM), whole(VMEM), whole(pl.ANY)],
        out_specs=whole(VMEM),
        compiler_params=params(8),
        name="bias",
    )(meta, table, other)


def tile_kernel(full_ref, out):
    for i in range(2):
        out[i] = full_ref[i]


def tile_of(full):
    return pl.pallas_call(
        tile_kernel,
        out_shape=jax.ShapeDtypeStruct((2,) + full.shape[1:], BF16),
        in_specs=[whole(VMEM)],
        out_specs=whole(VMEM),
        compiler_params=params(8),
        name="tile",
    )(full)


def stack_kernel(count, *refs):
    for i in range(count):
        for j in range(2):
            refs[-1][i, j] = refs[i][j]


def stack(parts, *others):
    one = parts[0].shape
    return pl.pallas_call(
        functools.partial(stack_kernel, len(parts)),
        out_shape=jax.ShapeDtypeStruct((len(parts), 2) + one[1:], BF16),
        in_specs=[whole(VMEM)] * len(parts) + [whole(pl.ANY)] * len(others),
        out_specs=whole(VMEM),
        compiler_params=params(8),
        name="stack",
    )(*parts, *others)


def after_kernel(*refs):
    pass


def after(x, *others):
    return pl.pallas_call(
        after_kernel,
        out_shape=jax.ShapeDtypeStruct(x.shape, x.dtype),
        in_specs=[whole(pl.ANY)] * (1 + len(others)),
        out_specs=whole(pl.ANY),
        input_output_aliases={0: 0},
        compiler_params=params(1),
        name="after",
    )(x, *others)


class Sizes:
    def __init__(self, shards, replicas, tiles, own_heads, width, tok):
        self.shards, self.replicas, self.tiles = shards, replicas, tiles
        self.own_heads, self.width, self.tok = own_heads, width, tok
        self.groups = shards * replicas
        self.batch = own_heads if self.groups <= 8 else 1
        self.inv_root = 1.0 / math.sqrt(width)

    def group_of(self, meta_ref, turn, hop):
        return (meta_ref[0] ^ hop) * self.replicas + lax.rem(meta_ref[1] + turn, self.replicas)

    def span(self, meta_ref, turn, hop):
        return meta_ref[3 + self.group_of(meta_ref, turn, hop)]

    def level(self, meta_ref, span):
        return meta_ref[3 + self.groups + span]

    def live(self, meta_ref, hop):
        tile = self.group_of(meta_ref, 0, hop) * self.tiles + meta_ref[2]
        return meta_ref[3 + 2 * self.groups + tile]

    def slots(self, meta_ref):
        for turn in range(self.replicas):
            for hop in range(self.shards):
                yield turn, hop, self.span(meta_ref, turn, hop)

    def lanes(self, h):
        return pl.ds(h * self.width, self.width)

    def first_head(self, meta_ref):
        base = 0 if self.batch == self.own_heads else pl.program_id(0) * self.batch
        return meta_ref[0] * self.own_heads + base

    def steps(self, count):
        return lax.div(count + 1, 2)

    def call(self, kernel, name, limit, operands, outs, scratch):
        split = self.batch != self.own_heads

        def spec(shape, kind):
            if kind == "scalar":
                return whole(SMEM)
            if not split:
                return whole(VMEM)
            block, axis = list(shape), {"heads": 0, "lanes": len(shape) - 1}.get(kind)
            if axis is None:
                return pl.BlockSpec(tuple(block), lambda h: (0,) * len(block))
            block[axis] = block[axis] // self.own_heads * self.batch
            return pl.BlockSpec(
                tuple(block), lambda h: tuple(h if d == axis else 0 for d in range(len(block)))
            )

        return pl.pallas_call(
            functools.partial(kernel, self),
            grid=(self.own_heads // self.batch,) if split else (),
            in_specs=[spec(x.shape, kind) for x, kind in operands],
            out_specs=[spec(x.shape, kind) for x, kind in outs],
            out_shape=[x for x, kind in outs],
            scratch_shapes=scratch,
            compiler_params=params(limit),
            name=name,
        )(*(x for x, kind in operands))


def by_slot(z, refs):
    found = []
    for turn in range(len(refs) // 3):
        first, middle, last = refs[3 * turn : 3 * turn + 3]
        found += [first] + [middle.at[i] for i in range(z.shards - 2)] + [last]
    return found


def order_tiles(z, meta_ref, tiles, kv, kt, vt):
    for turn, hop, span in z.slots(meta_ref):
        ref = tiles[turn * z.shards + hop]
        rows = pl.ds(pl.multiple_of(span * z.tok, z.tok), z.tok)
        half = pl.ds(pl.multiple_of(lax.rem(span, 2) * z.tok, z.tok), z.tok)
        for h in range(z.batch):
            k, v = ref[0, :, z.lanes(h)], ref[1, :, z.lanes(h)]
            kv[h, rows, : z.width] = k
            kv[h, rows, z.width :] = v
            kt[h, lax.div(span, 2), :, half] = k.T
            vt[h, lax.div(span, 2), :, half] = v.T


def softmax_sums(z, first, count, bias, kv, both, score, dprob):
    heads, tok = range(z.batch), z.tok
    scale = z.inv_root * LOG2E

    def step(c, carry):
        rows = pl.ds(pl.multiple_of(c * 2 * tok, 2 * tok), 2 * tok)
        new = []
        for h in heads:
            sd = jnp.dot(kv[h, rows, :], both[h][...], preferred_element_type=F32)
            parts = []
            for j in range(2):
                span = 2 * c + j
                shift = bias[span, pl.ds(first + h, 1), :] + jnp.where(span < count, 0.0, DEAD)
                parts.append(sd[j * tok : (j + 1) * tok, :tok] * scale + shift)
            s, dp = jnp.concatenate(parts, axis=0), sd[:, tok:]
            score[h][c] = s
            dprob[h][c] = dp
            old, total, mixed = carry[3 * h : 3 * h + 3]
            peak = jnp.maximum(old, fold(jnp.max, s))
            e = jnp.exp2(s.reshape(-1, 8, tok) - peak[None])
            fade = jnp.exp2(old - peak)
            new += [
                peak,
                total * fade + jnp.sum(e, axis=0),
                mixed * fade + jnp.sum(e * dp.reshape(-1, 8, tok), axis=0),
            ]
        return tuple(new)

    start = (jnp.full((8, tok), -3e38, F32), jnp.zeros((8, tok), F32), jnp.zeros((8, tok), F32))
    sums = lax.fori_loop(0, z.steps(count), step, start * z.batch)
    peaks = [jnp.max(x, axis=0, keepdims=True) for x in sums[::3]]
    fades = [jnp.exp2(x - peak) for x, peak in zip(sums[::3], peaks)]
    totals, mixed = (
        [jnp.sum(x * fade, axis=0, keepdims=True) for x, fade in zip(sums[i::3], fades)]
        for i in (1, 2)
    )
    return peaks, totals, mixed


def gradients(z, count, log_total, delta, score, dprob, both, kt, vt, acc, ot, dqt):
    def grad_step(c, carry):
        rows = pl.ds(pl.multiple_of(c * 2 * z.tok, 2 * z.tok), 2 * z.tok)
        for h in range(z.batch):
            w = jnp.exp2(score[h][c] - log_total[h])
            ds = (w * (dprob[h][c] - delta[h])).astype(BF16)
            w = w.astype(BF16)
            acc[h, rows, :] += jnp.dot(
                jnp.concatenate([ds, w], axis=1), both[h][...], preferred_element_type=F32
            )
            ot[h][...] += jnp.dot(vt[h, c], w, preferred_element_type=F32)
            dqt[h][...] += jnp.dot(kt[h, c], ds, preferred_element_type=F32)
        return carry

    lax.fori_loop(0, z.steps(count), grad_step, 0)


def write_sums(z, meta_ref, acc, sums):
    for turn, hop, span in z.slots(meta_ref):
        goal = sums[turn * z.shards + hop]
        rows = pl.ds(pl.multiple_of(span * z.tok, z.tok), z.tok)
        for h in range(z.batch):
            goal[0, :, z.lanes(h)] = (acc[h, rows, : z.width] * z.inv_root).astype(BF16)
            goal[1, :, z.lanes(h)] = acc[h, rows, z.width :].astype(BF16)


def own_kernel(z, meta_ref, bias, *refs):
    full, refs = refs[: z.shards], refs[z.shards :]
    count = 3 * (z.replicas - 1)
    others, (kt, vt, both, turned, score, dprob, stats, kv) = refs[:count], refs[count:]
    first = z.first_head(meta_ref)
    order_tiles(z, meta_ref, list(full) + by_slot(z, others), kv, kt, vt)
    for hop in range(z.shards):
        for h in range(z.batch):
            for i in range(2):
                for j in range(2):
                    block = full[hop][2 + i, :, z.lanes(h)]
                    block = block if i == j else jnp.zeros_like(block)
                    both[h, hop, pl.ds(i * z.tok, z.tok), z.lanes(j)] = block
                    turned[h, hop, pl.ds(i * z.width, z.width), pl.ds(j * z.tok, z.tok)] = block.T
        count = z.span(meta_ref, 0, hop) + 1
        heads = range(z.batch)
        sums = softmax_sums(
            z,
            first,
            count,
            bias,
            kv,
            [turned.at[h, hop] for h in heads],
            [score.at[h, hop] for h in heads],
            [dprob.at[h, hop] for h in heads],
        )
        for h in heads:
            for i in range(3):
                stats[h, hop, i : i + 1, :] = sums[i][h]


def ahead_kernel(z, meta_ref, bias, both, turned, stats, *refs):
    tiles, refs = by_slot(z, refs[: 3 * z.replicas]), refs[3 * z.replicas :]
    (final, ot, dqt), sums, refs = refs[:3], refs[3 : 3 + z.groups], refs[3 + z.groups :]
    kv, kt, vt, score, dprob, acc = refs
    first = z.first_head(meta_ref)
    heads = range(z.batch)
    order_tiles(z, meta_ref, tiles, kv, kt, vt)
    acc[...] = jnp.zeros_like(acc)
    ot[...] = jnp.zeros_like(ot)
    dqt[...] = jnp.zeros_like(dqt)
    for hop in range(z.shards):
        count = z.span(meta_ref, 0, hop) + 1
        live = z.live(meta_ref, hop)
        near = [[stats[h, hop, i : i + 1, :] for h in heads] for i in range(3)]

        @pl.when(live != 1)
        def _():
            for h in heads:
                final[h, hop, 0:1, :] = near[0][h] + jnp.log2(near[1][h])
                final[h, hop, 1:2, :] = near[2][h] / near[1][h]

        @pl.when(live == 1)
        def _():
            views = (
                [score.at[h] for h in heads],
                [dprob.at[h] for h in heads],
                [both.at[h, hop] for h in heads],
            )
            far = softmax_sums(z, first, count, bias, kv, [turned.at[h, hop] for h in heads], views[0], views[1])
            log_total, delta = [], []
            for h in heads:
                peak = jnp.maximum(near[0][h], far[0][h])
                a, b = jnp.exp2(near[0][h] - peak), jnp.exp2(far[0][h] - peak)
                total = near[1][h] * a + far[1][h] * b
                log_total.append(peak + jnp.log2(total))
                delta.append((near[2][h] * a + far[2][h] * b) / total)
                final[h, hop, 0:1, :] = log_total[h]
                final[h, hop, 1:2, :] = delta[h]
            gradients(
                z,
                count,
                log_total,
                delta,
                *views,
                kt,
                vt,
                acc,
                [ot.at[h, hop] for h in heads],
                [dqt.at[h, hop] for h in heads],
            )

    write_sums(z, meta_ref, acc, sums)


def rows_kernel(z, meta_ref, kt, vt, both, score, dprob, final, ot_in, dqt_in, *refs):
    refs = refs[1:]
    rows_out, sums, refs = refs[: z.shards], refs[z.shards : z.shards + z.groups], refs[-3:]
    acc, ot, dqt = refs
    heads = range(z.batch)
    acc[...] = jnp.zeros_like(acc)
    for hop in range(z.shards):
        count = z.span(meta_ref, 0, hop) + 1
        for h in heads:
            ot[h] = ot_in[h, hop]
            dqt[h] = dqt_in[h, hop]
        gradients(
            z,
            count,
            [final[h, hop, 0:1, :] for h in heads],
            [final[h, hop, 1:2, :] for h in heads],
            [score.at[h, hop] for h in heads],
            [dprob.at[h, hop] for h in heads],
            [both.at[h, hop] for h in heads],
            kt,
            vt,
            acc,
            [ot.at[h] for h in heads],
            [dqt.at[h] for h in heads],
        )
        for h in heads:
            rows_out[hop][0, :, z.lanes(h)] = ot[h].astype(BF16).T
            rows_out[hop][1, :, z.lanes(h)] = (dqt[h] * z.inv_root).astype(BF16).T
    write_sums(z, meta_ref, acc, sums)


def add_up(terms, at=()):
    total = terms[0][at].astype(F32)
    for term in terms[1:]:
        total = total + term[at].astype(F32)
    return total.astype(BF16)


def join(lists):
    count = len(lists[0])

    def kernel(*refs):
        for i in range(len(lists)):
            for which in range(2):
                refs[-1][i, which] = add_up(refs[i * count : (i + 1) * count], which)

    operands = [x for parts in lists for x in parts]
    return pl.pallas_call(
        kernel,
        out_shape=jax.ShapeDtypeStruct((len(lists),) + operands[0].shape, BF16),
        in_specs=[whole(VMEM)] * len(operands),
        out_specs=whole(VMEM),
        compiler_params=params(8),
        name="join",
    )(*operands)


def merge(lists, joined, last):
    count = len(lists[0])

    def kernel(*refs):
        refs, outs = refs[: -1 - len(lists)], refs[-1 - len(lists) :]
        arrived, refs = refs[0], refs[1:]
        for which in range(2):
            for i in range(len(lists)):
                terms = list(refs[i * count : (i + 1) * count]) + [arrived.at[i]]
                outs[i][which] = add_up(terms, which)
            outs[-1][which] = add_up(refs[len(lists) * count :], which)

    operands = [joined] + [x for parts in lists for x in parts] + last
    return pl.pallas_call(
        kernel,
        out_shape=[jax.ShapeDtypeStruct(last[0].shape, BF16)] * (len(lists) + 1),
        in_specs=[whole(VMEM)] * len(operands),
        out_specs=[whole(VMEM)] * (len(lists) + 1),
        compiler_params=params(8),
        name="merge",
    )(*operands)


def unpack(pos, lists):
    shards = len(lists)
    tok, cols = lists[0][0].shape[1:]

    def kernel(pos_ref, *refs):
        ins, outs = list(refs[:-2]), refs[-2:]
        for hop in range(shards):
            terms, ins = ins[: len(lists[hop])], ins[len(lists[hop]) :]
            lanes = pl.ds(pl.multiple_of((pos_ref[0] ^ hop) * cols, 128), cols)
            for i in range(2):
                outs[i][:, lanes] = add_up(terms, i)

    operands = [x for parts in lists for x in parts]
    return pl.pallas_call(
        kernel,
        out_shape=[jax.ShapeDtypeStruct((tok, cols * shards), BF16)] * 2,
        in_specs=[whole(SMEM)] + [whole(VMEM)] * len(operands),
        out_specs=[whole(VMEM)] * 2,
        compiler_params=params(8),
        name="unpack",
    )(pos, *operands)


def per_device(queries, keys, values, grad_out, span_of_group, noise_level, next_live, level_bias):
    tok, model = queries.shape
    heads = level_bias.shape[1]
    width = model // heads
    groups = lax.axis_size("tm")
    tiles = lax.axis_size("tile")
    shards = shard_count(heads, groups)
    replicas = groups // shards
    own = heads // shards
    cols = own * width
    z = Sizes(shards, replicas, tiles, own, width, tok)
    me = lax.axis_index("tm")
    pos = jnp.stack([me // replicas, me % replicas, lax.axis_index("tile")]).astype(jnp.int32)
    meta = jnp.concatenate([pos, span_of_group, noise_level, next_live])
    shape = jax.ShapeDtypeStruct

    def to_shard(x, hop, lift):
        if hop == 0 and lift == 0:
            return x
        pairs = []
        for t in range(groups):
            goal = ((t // replicas) ^ hop) * replicas + t % replicas
            for s in range(tiles):
                pairs.append((t * tiles + s, goal * tiles + (s + lift) % tiles))
        return lax.ppermute(x, ("tm", "tile"), pairs)

    def to_replica(x, turn):
        pairs = [(t, t // replicas * replicas + (t - turn) % replicas) for t in range(groups)]
        return lax.ppermute(x, "tm", pairs)

    def with_others(parts):
        return [
            [parts[hop]]
            + [
                to_replica(parts[turn * shards + hop], replicas - turn)
                for turn in range(1, replicas)
            ]
            for hop in hops
        ]

    def swapped(tiles):
        return [to_replica(x, turn) for turn in range(1, replicas) for x in tiles]

    hops = list(range(shards))
    last = shards - 1
    packed, pair, early = pack(z, pos, (keys, values, queries, grad_out))
    full = [to_shard(packed[hop], hop, 0) for hop in hops]
    bias = bias_rows(z, meta, level_bias.T, full[1])
    far_first, far_last = to_shard(pair, 0, -1), to_shard(early, 0, -1)
    direct = stack(full[1:last], far_first, far_last, bias)
    near = [pair, direct, tile_of(full[last])]
    far = [far_first, to_shard(direct, 0, -1), to_shard(far_last, last, 0)]

    scalars = [(meta, "scalar")]
    one = shape((2, tok, cols), BF16)
    half = groups // 2
    square = shape((own, half, width, 2 * tok), BF16)
    block = shape((own, shards, half, 2 * tok, tok), F32)
    stat = shape((own, shards, 8, tok), F32)
    part = shape((own, shards, width, tok), F32)
    batch = z.batch
    kt, vt, both, turned, score, dprob, stats = z.call(
        own_kernel,
        "own",
        8 if batch == own else 48,
        scalars
        + [(bias, "all")]
        + [(x, "lanes") for x in full + swapped(near)],
        [
            (square, "heads"),
            (square, "heads"),
            (shape((own, shards, 2 * tok, 2 * width), BF16), "heads"),
            (shape((own, shards, 2 * width, 2 * tok), BF16), "heads"),
            (block, "heads"),
            (block, "heads"),
            (stat, "heads"),
        ],
        [
            VMEM((batch, groups * tok, 2 * width), BF16),
        ],
    )
    far = [after(x, stats) for x in far]
    far += swapped(far)
    results = z.call(
        ahead_kernel,
        "ahead",
        16 if batch == own else 48,
        scalars
        + [(bias, "all"), (both, "heads"), (turned, "heads"), (stats, "heads")]
        + [(x, "lanes") for x in far],
        [(stat, "heads"), (part, "heads"), (part, "heads")]
        + [(one, "lanes")] * groups,
        [
            VMEM((batch, groups * tok, 2 * width), BF16),
            VMEM((batch, half, width, 2 * tok), BF16),
            VMEM((batch, half, width, 2 * tok), BF16),
            VMEM((batch, half, 2 * tok, tok), F32),
            VMEM((batch, half, 2 * tok, tok), F32),
            VMEM((batch, groups * tok, 2 * width), F32),
        ],
    )
    final, ot, dqt = results[:3]
    far_parts = with_others(results[3:])
    far_sums = join(far_parts[1:])
    far_home = to_shard(far_sums, 0, 1)
    results = z.call(
        rows_kernel,
        "rows",
        8 if batch == own else 48,
        scalars
        + [(x, "heads") for x in (kt, vt, both, score, dprob, final, ot, dqt)]
        + [(far_sums, "lanes")],
        [(one, "lanes")] * (shards + groups),
        [
            VMEM((batch, groups * tok, 2 * width), F32),
            VMEM((batch, width, tok), F32),
            VMEM((batch, width, tok), F32),
        ],
    )
    rows_home = [to_shard(results[hop], hop, 0) for hop in hops]
    near_parts = with_others(results[shards:])
    *sums, far_last = merge(near_parts[1:], far_home, far_parts[0])
    sums_home = [to_shard(x, hop, 0) for hop, x in zip(hops[1:], sums)]
    last_home = to_shard(far_last, 0, 1)
    attended, grad_queries = unpack(pos, [[x] for x in rows_home])
    grad_keys, grad_values = unpack(
        pos, [near_parts[0] + [last_home]] + [[x] for x in sums_home]
    )
    return attended, grad_queries, grad_keys, grad_values


def solution(mesh):
    sharded = P(("tm", "tile"), None)
    return jax.shard_map(
        per_device,
        mesh=mesh,
        in_specs=(sharded,) * 4 + (P(),) * 4,
        out_specs=(sharded,) * 4,
        check_vma=False,
    )
```

```python
import functools
import math

import jax
import jax.numpy as jnp
from jax import lax
from jax.experimental import pallas as pl
from jax.experimental.pallas import tpu as pltpu
from jax.sharding import PartitionSpec as P

VMEM = pltpu.VMEM
SMEM = pltpu.SMEM
BF16 = jnp.bfloat16
F32 = jnp.float32
NT = (((1,), (1,)), ((), ()))
LOG2E = 1.4426950408889634
DEAD = -1e30


def params(mib):
    return pltpu.CompilerParams(vmem_limit_bytes=mib * 1024 * 1024)


def whole(space):
    return pl.BlockSpec(memory_space=space)


def shard_count(heads, groups):
    count = 1
    while heads % (2 * count) == 0 and groups % (2 * count) == 0:
        count *= 2
    return count


def fold(op, x):
    return op(x.reshape(x.shape[0] // 8, 8, x.shape[1]), axis=0)


def pack_kernel(z, pos_ref, *refs):
    sources, refs = refs[:4], refs[4:]
    outs, (pair, pair_rows, early, held, sems) = refs[: z.shards], refs[z.shards :]
    half, cols = z.tok // 2, z.own_heads * z.width
    copies = []
    for i, src in enumerate(sources):
        for j in range(2):
            rows = pl.ds(j * half, half)
            copy = pltpu.make_async_copy(src.at[rows], held.at[i, rows], sems.at[i, j])
            copy.start()
            copies.append(copy)
    for i in range(4):
        copies[2 * i].wait()
        copies[2 * i + 1].wait()
        for hop in range(z.shards):
            lanes = pl.ds(pl.multiple_of((pos_ref[0] ^ hop) * cols, 128), cols)
            part = held[i, :, lanes]
            outs[hop][i] = part
            if hop == 0:
                (pair if i < 2 else pair_rows)[i % 2] = part
            if hop == z.shards - 1 and i < 2:
                early[i] = part


def pack(z, pos, arrays):
    cols = z.own_heads * z.width
    sources = [pltpu.with_memory_space_constraint(x, pltpu.HBM) for x in arrays]
    shape = jax.ShapeDtypeStruct
    results = pl.pallas_call(
        functools.partial(pack_kernel, z),
        out_shape=[shape((4, z.tok, cols), BF16)] * z.shards
        + [shape((2, z.tok, cols), BF16)] * 3,
        in_specs=[whole(SMEM)] + [whole(pltpu.HBM)] * 4,
        out_specs=[whole(VMEM)] * (z.shards + 3),
        scratch_shapes=[
            VMEM((4, z.tok, cols * z.shards), BF16),
            pltpu.SemaphoreType.DMA((4, 2)),
        ],
        compiler_params=params(8),
        name="pack",
    )(pos, *sources)
    return results[:-3], results[-3:]


def bias_kernel(z, meta_ref, table_ref, after_ref, bias):
    level_ids = lax.broadcasted_iota(jnp.int32, table_ref.shape, 1)
    for span in range(z.groups):
        column = jnp.sum(
            jnp.where(level_ids == z.level(meta_ref, span), table_ref[...], 0.0),
            axis=1,
            keepdims=True,
        )
        bias[span] = jnp.broadcast_to(column * LOG2E, bias.shape[1:])


def bias_rows(z, meta, table, other):
    return pl.pallas_call(
        functools.partial(bias_kernel, z),
        out_shape=jax.ShapeDtypeStruct((z.groups, table.shape[0], z.tok), F32),
        in_specs=[whole(SMEM), whole(VMEM), whole(pl.ANY)],
        out_specs=whole(VMEM),
        compiler_params=params(8),
        name="bias",
    )(meta, table, other)


def stack_kernel(count, base, *refs):
    out = refs[-1]
    for i in range(count):
        for j in range(2):
            if len(out.shape) == 4:
                out[i, j] = refs[i][base + j]
            else:
                out[j] = refs[i][base + j]


def stack(parts, base, others=(), flat=False):
    one = (2,) + parts[0].shape[1:]
    return pl.pallas_call(
        functools.partial(stack_kernel, len(parts), base),
        out_shape=jax.ShapeDtypeStruct(one if flat else (len(parts),) + one, BF16),
        in_specs=[whole(VMEM)] * len(parts) + [whole(pl.ANY)] * len(others),
        out_specs=whole(VMEM),
        compiler_params=params(8),
        name="stack",
    )(*parts, *others)


def after_kernel(*refs):
    pass


def after(x, *others):
    return pl.pallas_call(
        after_kernel,
        out_shape=jax.ShapeDtypeStruct(x.shape, x.dtype),
        in_specs=[whole(pl.ANY)] * (1 + len(others)),
        out_specs=whole(pl.ANY),
        input_output_aliases={0: 0},
        compiler_params=params(1),
        name="after",
    )(x, *others)


class Sizes:
    def __init__(self, shards, replicas, tiles, own_heads, width, tok):
        self.shards, self.replicas, self.tiles = shards, replicas, tiles
        self.own_heads, self.width, self.tok = own_heads, width, tok
        self.groups = shards * replicas
        self.batch = own_heads if self.groups <= 8 else 1
        self.inv_root = 1.0 / math.sqrt(width)

    def group_of(self, meta_ref, turn, hop):
        return (meta_ref[0] ^ hop) * self.replicas + lax.rem(meta_ref[1] + turn, self.replicas)

    def span(self, meta_ref, turn, hop):
        return meta_ref[3 + self.group_of(meta_ref, turn, hop)]

    def level(self, meta_ref, span):
        return meta_ref[3 + self.groups + span]

    def live(self, meta_ref, turn, hop):
        tile = self.group_of(meta_ref, turn, hop) * self.tiles + meta_ref[2]
        return meta_ref[3 + 2 * self.groups + tile]

    def ranks(self, meta_ref, ahead):
        turn = self.replicas - 1 if ahead else 0
        spans = [self.span(meta_ref, turn, hop) for hop in range(self.shards)]
        return spans, [sum(jnp.where(x < span, 1, 0) for x in spans) for span in spans]

    def queries(self, meta_ref, ahead):
        spans, _ = self.ranks(meta_ref, ahead)
        for turn in range(self.replicas):
            for hop in range(self.shards):
                span = self.span(meta_ref, turn, hop)
                count = sum(jnp.where(x <= span, 1, 0) for x in spans)
                yield turn * self.shards + hop, count, self.live(meta_ref, turn, hop)

    def lanes(self, h):
        return pl.ds(h * self.width, self.width)

    def first_head(self, meta_ref):
        base = 0 if self.batch == self.own_heads else pl.program_id(0) * self.batch
        return meta_ref[0] * self.own_heads + base

    def steps(self, count):
        return lax.div(count + 1, 2)

    def call(self, kernel, name, limit, operands, outs, scratch):
        split = self.batch != self.own_heads

        def spec(shape, kind):
            if kind == "scalar":
                return whole(SMEM)
            if not split:
                return whole(VMEM)
            block, axis = list(shape), {"heads": 0, "lanes": len(shape) - 1}.get(kind)
            if axis is None:
                return pl.BlockSpec(tuple(block), lambda h: (0,) * len(block))
            block[axis] = block[axis] // self.own_heads * self.batch
            return pl.BlockSpec(
                tuple(block), lambda h: tuple(h if d == axis else 0 for d in range(len(block)))
            )

        return pl.pallas_call(
            functools.partial(kernel, self),
            grid=(self.own_heads // self.batch,) if split else (),
            in_specs=[spec(x.shape, kind) for x, kind in operands],
            out_specs=[spec(x.shape, kind) for x, kind in outs],
            out_shape=[x for x, kind in outs],
            scratch_shapes=scratch,
            compiler_params=params(limit),
            name=name,
        )(*(x for x, kind in operands))


def by_hop(z, refs):
    found = []
    for turn in range(len(refs) // 3):
        first, middle, last = refs[3 * turn : 3 * turn + 3]
        found += [first] + [middle.at[i] for i in range(z.shards - 2)] + [last]
    return found


def order_tiles(z, tiles, ranks, kv, kt, vt):
    for ref, rank in zip(tiles, ranks):
        rows = pl.ds(pl.multiple_of(rank * z.tok, z.tok), z.tok)
        half = pl.ds(pl.multiple_of(lax.rem(rank, 2) * z.tok, z.tok), z.tok)
        for h in range(z.batch):
            k, v = ref[0, :, z.lanes(h)], ref[1, :, z.lanes(h)]
            kv[h, rows, : z.width] = k
            kv[h, rows, z.width :] = v
            kt[h, lax.div(rank, 2), :, half] = k.T
            vt[h, lax.div(rank, 2), :, half] = v.T


def softmax_sums(z, first, count, bias, kv, both, score, dprob):
    heads, tok = range(z.batch), z.tok
    scale = z.inv_root * LOG2E

    def step(c, carry):
        rows = pl.ds(pl.multiple_of(c * 2 * tok, 2 * tok), 2 * tok)
        new = []
        for h in heads:
            sd = lax.dot_general(kv[h, rows, :], both[h][...], NT, preferred_element_type=F32)
            parts = []
            for j in range(2):
                rank = 2 * c + j
                shift = bias[rank, pl.ds(first + h, 1), :] + jnp.where(rank < count, 0.0, DEAD)
                parts.append(sd[j * tok : (j + 1) * tok, :tok] * scale + shift)
            s, dp = jnp.concatenate(parts, axis=0), sd[:, tok:]
            score[h][c] = s
            dprob[h][c] = dp
            old, total, mixed = carry[3 * h : 3 * h + 3]
            peak = jnp.maximum(old, fold(jnp.max, s))
            e = jnp.exp2(s.reshape(-1, 8, tok) - peak[None])
            fade = jnp.exp2(old - peak)
            new += [
                peak,
                total * fade + jnp.sum(e, axis=0),
                mixed * fade + jnp.sum(e * dp.reshape(-1, 8, tok), axis=0),
            ]
        return tuple(new)

    start = (jnp.full((8, tok), -3e38, F32), jnp.zeros((8, tok), F32), jnp.zeros((8, tok), F32))
    sums = lax.fori_loop(0, z.steps(count), step, start * z.batch)
    peaks = [jnp.max(x, axis=0, keepdims=True) for x in sums[::3]]
    fades = [jnp.exp2(x - peak) for x, peak in zip(sums[::3], peaks)]
    totals, mixed = (
        [jnp.sum(x * fade, axis=0, keepdims=True) for x, fade in zip(sums[i::3], fades)]
        for i in (1, 2)
    )
    return peaks, totals, mixed


def gradients(z, count, log_total, delta, score, dprob, both, kt, vt, acc, ot, dqt):
    def grad_step(c, carry):
        rows = pl.ds(pl.multiple_of(c * 2 * z.tok, 2 * z.tok), 2 * z.tok)
        for h in range(z.batch):
            w = jnp.exp2(score[h][c] - log_total[h])
            ds = (w * (dprob[h][c] - delta[h])).astype(BF16)
            w = w.astype(BF16)
            acc[h, rows, :] += jnp.dot(
                jnp.concatenate([ds, w], axis=1), both[h][...], preferred_element_type=F32
            )
            ot[h][...] += jnp.dot(vt[h, c], w, preferred_element_type=F32)
            dqt[h][...] += jnp.dot(kt[h, c], ds, preferred_element_type=F32)
        return carry

    lax.fori_loop(0, z.steps(count), grad_step, 0)


def write_sums(z, goals, ranks, acc):
    for goal, rank in zip(goals, ranks):
        rows = pl.ds(pl.multiple_of(rank * z.tok, z.tok), z.tok)
        for h in range(z.batch):
            goal[0, :, z.lanes(h)] = (acc[h, rows, : z.width] * z.inv_root).astype(BF16)
            goal[1, :, z.lanes(h)] = acc[h, rows, z.width :].astype(BF16)


def merge_sums(parts):
    merged = []
    for h in range(len(parts[0][0])):
        peak = parts[0][0][h]
        for part in parts[1:]:
            peak = jnp.maximum(peak, part[0][h])
        fades = [jnp.exp2(part[0][h] - peak) for part in parts]
        merged.append(
            [peak] + [sum(part[i][h] * fade for part, fade in zip(parts, fades)) for i in (1, 2)]
        )
    return merged


def read_sums(stats, heads, at):
    return [[stats[h, at, i : i + 1, :] for h in heads] for i in range(3)]


def own_kernel(z, meta_ref, bias, *refs):
    full, refs = refs[: z.shards], refs[z.shards :]
    count = 3 * (z.replicas - 1)
    others, (kt, vt, both, score, dprob, stats, kv, ranked) = by_hop(z, refs[:count]), refs[count:]
    first = z.first_head(meta_ref)
    heads = range(z.batch)
    spans, ranks = z.ranks(meta_ref, False)
    order_tiles(z, full, ranks, kv, kt, vt)
    for span, rank in zip(spans, ranks):
        ranked[rank] = bias[span]
    for at, count, _ in z.queries(meta_ref, False):
        for h in heads:
            for i in range(2):
                for j in range(2):
                    ref, base = (full[at], 2) if at < z.shards else (others[at - z.shards], 0)
                    block = ref[base + i, :, z.lanes(h)]
                    both[h, at, pl.ds(i * z.tok, z.tok), z.lanes(j)] = (
                        block if i == j else jnp.zeros_like(block)
                    )
        sums = softmax_sums(
            z,
            first,
            count,
            ranked,
            kv,
            [both.at[h, at] for h in heads],
            [score.at[h, at] for h in heads],
            [dprob.at[h, at] for h in heads],
        )
        for h in heads:
            for i in range(3):
                stats[h, at, i : i + 1, :] = sums[i][h]


def ahead_kernel(z, meta_ref, bias, both, stats, *refs):
    tiles, (merged, kt, vt, score, dprob, kv, ranked) = by_hop(z, refs[:3]), refs[3:]
    first = z.first_head(meta_ref)
    heads = range(z.batch)
    spans, ranks = z.ranks(meta_ref, True)
    order_tiles(z, tiles, ranks, kv, kt, vt)
    for span, rank in zip(spans, ranks):
        ranked[rank] = bias[span]
    for at, count, live in z.queries(meta_ref, True):
        merged[:, at] = stats[:, at]

        @pl.when(live == 1)
        def _():
            far = softmax_sums(
                z,
                first,
                count,
                ranked,
                kv,
                [both.at[h, at] for h in heads],
                [score.at[h, at] for h in heads],
                [dprob.at[h, at] for h in heads],
            )
            sums = merge_sums([read_sums(stats, heads, at), far])
            for h in heads:
                for i in range(3):
                    merged[h, at, i : i + 1, :] = sums[h][i]


def back_kernel(z, meta_ref, both, stats, kt, vt, score, dprob, *refs):
    others, refs = refs[: z.replicas - 1], refs[z.replicas - 1 :]
    final, ot, dqt, own_sums, sums, acc = refs
    heads = range(z.batch)
    acc[...] = jnp.zeros_like(acc)
    ot[...] = jnp.zeros_like(ot)
    dqt[...] = jnp.zeros_like(dqt)
    for at, count, live in z.queries(meta_ref, True):
        parts = [read_sums(stats, heads, at)]
        for turn, other in enumerate(others, 1):
            place = (at // z.shards - turn) % z.replicas * z.shards + at % z.shards
            parts.append(read_sums(other, heads, place))
        log_total, delta = [], []
        for h, (peak, total, mixed) in enumerate(merge_sums(parts)):
            log_total.append(peak + jnp.log2(total))
            delta.append(mixed / total)
            final[h, at, 0:1, :] = log_total[h]
            final[h, at, 1:2, :] = delta[h]

        @pl.when(live == 1)
        def _():
            gradients(
                z,
                count,
                log_total,
                delta,
                [score.at[h, at] for h in heads],
                [dprob.at[h, at] for h in heads],
                [both.at[h, at] for h in heads],
                kt,
                vt,
                acc,
                [ot.at[h, at] for h in heads],
                [dqt.at[h, at] for h in heads],
            )

    goals = [own_sums] + [sums.at[i] for i in range(z.shards - 1)]
    write_sums(z, goals, z.ranks(meta_ref, True)[1], acc)


def rows_kernel(z, meta_ref, kt, vt, both, score, dprob, final, ot_in, dqt_in, *refs):
    rows_out, refs = refs[1 : 1 + z.groups], refs[1 + z.groups :]
    sums, (acc, ot, dqt) = refs[: z.shards], refs[z.shards :]
    heads = range(z.batch)
    acc[...] = jnp.zeros_like(acc)
    for at, count, _ in z.queries(meta_ref, False):
        for h in heads:
            ot[h] = ot_in[h, at]
            dqt[h] = dqt_in[h, at]
        gradients(
            z,
            count,
            [final[h, at, 0:1, :] for h in heads],
            [final[h, at, 1:2, :] for h in heads],
            [score.at[h, at] for h in heads],
            [dprob.at[h, at] for h in heads],
            [both.at[h, at] for h in heads],
            kt,
            vt,
            acc,
            [ot.at[h] for h in heads],
            [dqt.at[h] for h in heads],
        )
        for h in heads:
            rows_out[at][0, :, z.lanes(h)] = ot[h].astype(BF16).T
            rows_out[at][1, :, z.lanes(h)] = (dqt[h] * z.inv_root).astype(BF16).T
    write_sums(z, sums, z.ranks(meta_ref, False)[1], acc)


def add_up(terms, at=()):
    total = terms[0][at].astype(F32)
    for term in terms[1:]:
        total = total + term[at].astype(F32)
    return total.astype(BF16)


def add(lists):
    count = len(lists[0])

    def kernel(*refs):
        for i in range(len(lists)):
            for which in range(2):
                refs[i - len(lists)][which] = add_up(refs[i * count : (i + 1) * count], which)

    operands = [x for parts in lists for x in parts]
    return pl.pallas_call(
        kernel,
        out_shape=[jax.ShapeDtypeStruct(operands[0].shape, BF16)] * len(lists),
        in_specs=[whole(VMEM)] * len(operands),
        out_specs=[whole(VMEM)] * len(lists),
        compiler_params=params(8),
        name="add",
    )(*operands)


def merge(lists, joined, last):
    count = len(lists[0])

    def kernel(*refs):
        refs, outs = refs[: -1 - len(lists)], refs[-1 - len(lists) :]
        arrived, refs = refs[0], refs[1:]
        for which in range(2):
            for i in range(len(lists)):
                terms = list(refs[i * count : (i + 1) * count]) + [arrived.at[i]]
                outs[i][which] = add_up(terms, which)
            outs[-1][which] = add_up(refs[len(lists) * count :], which)

    operands = [joined] + [x for parts in lists for x in parts] + last
    return pl.pallas_call(
        kernel,
        out_shape=[jax.ShapeDtypeStruct(last[0].shape, BF16)] * (len(lists) + 1),
        in_specs=[whole(VMEM)] * len(operands),
        out_specs=[whole(VMEM)] * (len(lists) + 1),
        compiler_params=params(8),
        name="merge",
    )(*operands)


def unpack(pos, lists):
    shards = len(lists)
    tok, cols = lists[0][0].shape[1:]

    def kernel(pos_ref, *refs):
        ins, outs = list(refs[:-2]), refs[-2:]
        for hop in range(shards):
            terms, ins = ins[: len(lists[hop])], ins[len(lists[hop]) :]
            lanes = pl.ds(pl.multiple_of((pos_ref[0] ^ hop) * cols, 128), cols)
            for i in range(2):
                outs[i][:, lanes] = add_up(terms, i)

    operands = [x for parts in lists for x in parts]
    return pl.pallas_call(
        kernel,
        out_shape=[jax.ShapeDtypeStruct((tok, cols * shards), BF16)] * 2,
        in_specs=[whole(SMEM)] + [whole(VMEM)] * len(operands),
        out_specs=[whole(VMEM)] * 2,
        compiler_params=params(8),
        name="unpack",
    )(pos, *operands)


def per_device(queries, keys, values, grad_out, span_of_group, noise_level, next_live, level_bias):
    tok, model = queries.shape
    heads = level_bias.shape[1]
    width = model // heads
    groups = lax.axis_size("tm")
    tiles = lax.axis_size("tile")
    shards = shard_count(heads, groups)
    replicas = groups // shards
    own = heads // shards
    cols = own * width
    z = Sizes(shards, replicas, tiles, own, width, tok)
    me = lax.axis_index("tm")
    pos = jnp.stack([me // replicas, me % replicas, lax.axis_index("tile")]).astype(jnp.int32)
    meta = jnp.concatenate([pos, span_of_group, noise_level, next_live])
    shape = jax.ShapeDtypeStruct

    def to_shard(x, hop, lift):
        if hop == 0 and lift == 0:
            return x
        pairs = []
        for t in range(groups):
            goal = ((t // replicas) ^ hop) * replicas + (t - lift) % replicas
            for s in range(tiles):
                pairs.append((t * tiles + s, goal * tiles + (s + lift) % tiles))
        return lax.ppermute(x, ("tm", "tile"), pairs)

    def to_replica(x, turn):
        pairs = [(t, t // replicas * replicas + (t - turn) % replicas) for t in range(groups)]
        return lax.ppermute(x, "tm", pairs)

    def with_others(parts):
        return [
            [parts[hop]]
            + [
                to_replica(parts[turn * shards + hop], replicas - turn)
                for turn in range(1, replicas)
            ]
            for hop in hops
        ]

    def swapped(tiles):
        return [to_replica(x, turn) for turn in range(1, replicas) for x in tiles]

    hops = list(range(shards))
    last = shards - 1
    packed, (pair, pair_rows, early) = pack(z, pos, (keys, values, queries, grad_out))
    full = [to_shard(packed[hop], hop, 0) for hop in hops]
    far_first, far_last = to_shard(pair, 0, -1), to_shard(early, 0, -1)
    bias = bias_rows(z, meta, level_bias.T, far_first)
    direct = stack(full[1:last], 0, (far_first, far_last, bias))
    far = [far_first, to_shard(direct, 0, -1), to_shard(far_last, last, 0)]
    rows = swapped([pair_rows, stack(full[1:last], 2, (bias,)), stack(full[last:], 2, flat=True)])

    scalars = [(meta, "scalar")]
    half = shards // 2
    one = shape((2, tok, cols), BF16)
    square = shape((own, half, width, 2 * tok), BF16)
    block = shape((own, groups, half, 2 * tok, tok), F32)
    stat = shape((own, groups, 8, tok), F32)
    part = shape((own, groups, width, tok), F32)
    batch = z.batch
    limit = 8 if batch == own else 56
    tiles_scratch = VMEM((batch, shards * tok, 2 * width), BF16)
    ranked_scratch = VMEM((shards, heads, tok), F32)
    sums_scratch = VMEM((batch, shards * tok, 2 * width), F32)
    kt, vt, both, score, dprob, stats = z.call(
        own_kernel,
        "own",
        limit,
        scalars + [(bias, "all")] + [(x, "lanes") for x in full + rows],
        [
            (square, "heads"),
            (square, "heads"),
            (shape((own, groups, 2 * tok, 2 * width), BF16), "heads"),
            (block, "heads"),
            (block, "heads"),
            (stat, "heads"),
        ],
        [tiles_scratch, ranked_scratch],
    )
    merged, far_kt, far_vt, far_score, far_dprob = z.call(
        ahead_kernel,
        "ahead",
        limit,
        scalars
        + [(bias, "all"), (both, "heads"), (stats, "heads")]
        + [(after(x, stats), "lanes") for x in far],
        [
            (stat, "heads"),
            (square, "heads"),
            (square, "heads"),
            (block, "heads"),
            (block, "heads"),
        ],
        [tiles_scratch, ranked_scratch],
    )
    final, ot, dqt, first_sums, far_sums = z.call(
        back_kernel,
        "back",
        limit,
        scalars
        + [(x, "heads") for x in (both, merged, far_kt, far_vt, far_score, far_dprob)]
        + [(x, "heads") for x in swapped([merged])],
        [
            (stat, "heads"),
            (part, "heads"),
            (part, "heads"),
            (one, "lanes"),
            (shape((last, 2, tok, cols), BF16), "lanes"),
        ],
        [sums_scratch],
    )
    far_home = to_shard(far_sums, 0, 1)
    results = z.call(
        rows_kernel,
        "rows",
        limit,
        scalars
        + [(x, "heads") for x in (kt, vt, both, score, dprob, final, ot, dqt)]
        + [(first_sums, "lanes")],
        [(one, "lanes")] * (groups + shards),
        [sums_scratch, VMEM((batch, width, tok), F32), VMEM((batch, width, tok), F32)],
    )
    row_sums = add(with_others(results[:groups]))
    rows_home = [to_shard(row_sums[hop], hop, 0) for hop in hops]
    near_sums = results[groups:]
    *sums, first_late = merge([[x] for x in near_sums[1:]], far_home, [first_sums])
    sums_home = [to_shard(x, hop, 0) for hop, x in zip(hops[1:], sums)]
    first_home = to_shard(first_late, 0, 1)
    attended, grad_queries = unpack(pos, [[x] for x in rows_home])
    grad_keys, grad_values = unpack(
        pos, [[near_sums[0], first_home]] + [[x] for x in sums_home]
    )
    return attended, grad_queries, grad_keys, grad_values


def solution(mesh):
    sharded = P(("tm", "tile"), None)
    return jax.shard_map(
        per_device,
        mesh=mesh,
        in_specs=(sharded,) * 4 + (P(),) * 4,
        out_specs=(sharded,) * 4,
        check_vma=False,
    )
```

```python
import functools
import math

import jax
import jax.numpy as jnp
from jax import lax
from jax.experimental import pallas as pl
from jax.experimental.pallas import tpu as pltpu
from jax.sharding import PartitionSpec as P

VMEM = pltpu.VMEM
SMEM = pltpu.SMEM
BF16 = jnp.bfloat16
F32 = jnp.float32
NT = (((1,), (1,)), ((), ()))
LOG2E = 1.4426950408889634
DEAD = -1e30


def params(mib):
    return pltpu.CompilerParams(vmem_limit_bytes=mib * 1024 * 1024)


def whole(space):
    return pl.BlockSpec(memory_space=space)


def shard_count(heads, groups):
    count = 1
    while heads % (2 * count) == 0 and groups % (2 * count) == 0:
        count *= 2
    return count


def fold(op, x):
    return op(x.reshape(x.shape[0] // 8, 8, x.shape[1]), axis=0)


def pack_kernel(z, pos_ref, *refs):
    sources, refs = refs[:4], refs[4:]
    outs, (pair, early, held, sems) = refs[: z.shards], refs[z.shards :]
    half, cols = z.tok // 2, z.own_heads * z.width
    copies = []
    for i, src in enumerate(sources):
        for j in range(2):
            rows = pl.ds(j * half, half)
            copy = pltpu.make_async_copy(src.at[rows], held.at[i, rows], sems.at[i, j])
            copy.start()
            copies.append(copy)
    for i in range(4):
        copies[2 * i].wait()
        copies[2 * i + 1].wait()
        for hop in range(z.shards):
            lanes = pl.ds(pl.multiple_of((pos_ref[0] ^ hop) * cols, 128), cols)
            part = held[i, :, lanes]
            outs[hop][i] = part
            if hop == 0 and i < 2:
                pair[i] = part
            if hop == z.shards - 1 and i < 2:
                early[i] = part


def pack(z, pos, arrays):
    cols = z.own_heads * z.width
    sources = [pltpu.with_memory_space_constraint(x, pltpu.HBM) for x in arrays]
    shape = jax.ShapeDtypeStruct
    results = pl.pallas_call(
        functools.partial(pack_kernel, z),
        out_shape=[shape((4, z.tok, cols), BF16)] * z.shards
        + [shape((2, z.tok, cols), BF16)] * 2,
        in_specs=[whole(SMEM)] + [whole(pltpu.HBM)] * 4,
        out_specs=[whole(VMEM)] * (z.shards + 2),
        scratch_shapes=[
            VMEM((4, z.tok, cols * z.shards), BF16),
            pltpu.SemaphoreType.DMA((4, 2)),
        ],
        compiler_params=params(8),
        name="pack",
    )(pos, *sources)
    return results[:-2], results[-2:]


def bias_kernel(z, meta_ref, table_ref, after_ref, bias):
    level_ids = lax.broadcasted_iota(jnp.int32, table_ref.shape, 1)
    for span in range(z.groups):
        column = jnp.sum(
            jnp.where(level_ids == z.level(meta_ref, span), table_ref[...], 0.0),
            axis=1,
            keepdims=True,
        )
        bias[span] = jnp.broadcast_to(column * LOG2E, bias.shape[1:])


def bias_rows(z, meta, table, other):
    return pl.pallas_call(
        functools.partial(bias_kernel, z),
        out_shape=jax.ShapeDtypeStruct((z.groups, table.shape[0], z.tok), F32),
        in_specs=[whole(SMEM), whole(VMEM), whole(pl.ANY)],
        out_specs=whole(VMEM),
        compiler_params=params(8),
        name="bias",
    )(meta, table, other)


def stack_kernel(count, base, *refs):
    out = refs[-1]
    for i in range(count):
        for j in range(2):
            if len(out.shape) == 4:
                out[i, j] = refs[i][base + j]
            else:
                out[j] = refs[i][base + j]


def stack(parts, base, others=(), flat=False):
    one = (2,) + parts[0].shape[1:]
    return pl.pallas_call(
        functools.partial(stack_kernel, len(parts), base),
        out_shape=jax.ShapeDtypeStruct(one if flat else (len(parts),) + one, BF16),
        in_specs=[whole(VMEM)] * len(parts) + [whole(pl.ANY)] * len(others),
        out_specs=whole(VMEM),
        compiler_params=params(8),
        name="stack",
    )(*parts, *others)


def after_kernel(*refs):
    pass


def after(x, *others):
    return pl.pallas_call(
        after_kernel,
        out_shape=jax.ShapeDtypeStruct(x.shape, x.dtype),
        in_specs=[whole(pl.ANY)] * (1 + len(others)),
        out_specs=whole(pl.ANY),
        input_output_aliases={0: 0},
        compiler_params=params(1),
        name="after",
    )(x, *others)


class Sizes:
    def __init__(self, shards, replicas, tiles, own_heads, width, tok):
        self.shards, self.replicas, self.tiles = shards, replicas, tiles
        self.own_heads, self.width, self.tok = own_heads, width, tok
        self.groups = shards * replicas
        self.batch = own_heads if self.groups <= 8 else 1
        self.inv_root = 1.0 / math.sqrt(width)

    def group_of(self, meta_ref, turn, hop):
        return (meta_ref[0] ^ hop) * self.replicas + lax.rem(meta_ref[1] + turn, self.replicas)

    def span(self, meta_ref, turn, hop):
        return meta_ref[3 + self.group_of(meta_ref, turn, hop)]

    def level(self, meta_ref, span):
        return meta_ref[3 + self.groups + span]

    def live(self, meta_ref, turn, hop):
        tile = self.group_of(meta_ref, turn, hop) * self.tiles + meta_ref[2]
        return meta_ref[3 + 2 * self.groups + tile]

    def ranks(self, meta_ref, ahead):
        turn = self.replicas - 1 if ahead else 0
        spans = [self.span(meta_ref, turn, hop) for hop in range(self.shards)]
        return spans, [sum(jnp.where(x < span, 1, 0) for x in spans) for span in spans]

    def queries(self, meta_ref, ahead):
        spans, _ = self.ranks(meta_ref, ahead)
        for turn in range(self.replicas):
            for hop in range(self.shards):
                span = self.span(meta_ref, turn, hop)
                count = sum(jnp.where(x <= span, 1, 0) for x in spans)
                yield turn * self.shards + hop, count, self.live(meta_ref, turn, hop)

    def lanes(self, h):
        return pl.ds(h * self.width, self.width)

    def first_head(self, meta_ref):
        base = 0 if self.batch == self.own_heads else pl.program_id(0) * self.batch
        return meta_ref[0] * self.own_heads + base

    def blocks(self, count):
        for steps in range(1, self.shards // 2 + 1):
            yield 2 * steps * self.tok, lax.div(count + 1, 2) == steps

    def call(self, kernel, name, limit, operands, outs, scratch):
        split = self.batch != self.own_heads

        def spec(shape, kind):
            if kind == "scalar":
                return whole(SMEM)
            if not split:
                return whole(VMEM)
            block, axis = list(shape), {"heads": 0, "lanes": len(shape) - 1}.get(kind)
            if axis is None:
                return pl.BlockSpec(tuple(block), lambda h: (0,) * len(block))
            block[axis] = block[axis] // self.own_heads * self.batch
            return pl.BlockSpec(
                tuple(block), lambda h: tuple(h if d == axis else 0 for d in range(len(block)))
            )

        return pl.pallas_call(
            functools.partial(kernel, self),
            grid=(self.own_heads // self.batch,) if split else (),
            in_specs=[spec(x.shape, kind) for x, kind in operands],
            out_specs=[spec(x.shape, kind) for x, kind in outs],
            out_shape=[x for x, kind in outs],
            scratch_shapes=scratch,
            compiler_params=params(limit),
            name=name,
        )(*(x for x, kind in operands))


def by_hop(z, refs):
    found = []
    for turn in range(len(refs) // 3):
        first, middle, last = refs[3 * turn : 3 * turn + 3]
        found += [first] + [middle.at[i] for i in range(z.shards - 2)] + [last]
    return found


def order_tiles(z, tiles, ranks, kv, kt, vt):
    for ref, rank in zip(tiles, ranks):
        rows = pl.ds(pl.multiple_of(rank * z.tok, z.tok), z.tok)
        for h in range(z.batch):
            k, v = ref[0, :, z.lanes(h)], ref[1, :, z.lanes(h)]
            kv[h, rows, : z.width] = k
            kv[h, rows, z.width :] = v
            kt[h, :, rows] = k.T
            vt[h, :, rows] = v.T


def softmax_sums(z, first, count, rows, bias, kv, both, score, dprob):
    scale = z.inv_root * LOG2E
    sums = []
    for h in range(z.batch):
        sd = lax.dot_general(kv[h, :rows, :], both[h][...], NT, preferred_element_type=F32)
        parts = []
        for rank in range(rows // z.tok):
            shift = bias[rank, pl.ds(first + h, 1), :] + jnp.where(rank < count, 0.0, DEAD)
            parts.append(sd[rank * z.tok : (rank + 1) * z.tok, : z.tok] * scale + shift)
        s, dp = jnp.concatenate(parts, axis=0), sd[:, z.tok :]
        score[h][:rows, :] = s
        dprob[h][:rows, :] = dp
        peak = jnp.max(fold(jnp.max, s), axis=0, keepdims=True)
        e = jnp.exp2(s - peak)
        total = jnp.sum(fold(jnp.sum, e), axis=0, keepdims=True)
        mixed = jnp.sum(fold(jnp.sum, e * dp), axis=0, keepdims=True)
        sums.append((peak, total, mixed))
    return [[x[i] for x in sums] for i in range(3)]


def gradients(z, rows, log_total, delta, score, dprob, both, kt, vt, acc):
    found = []
    for h in range(z.batch):
        w = jnp.exp2(score[h][:rows, :] - log_total[h])
        ds = (w * (dprob[h][:rows, :] - delta[h])).astype(BF16)
        w = w.astype(BF16)
        acc[h, :rows, :] += jnp.dot(
            jnp.concatenate([ds, w], axis=1), both[h][...], preferred_element_type=F32
        )
        found.append(
            (
                jnp.dot(vt[h, :, :rows], w, preferred_element_type=F32),
                jnp.dot(kt[h, :, :rows], ds, preferred_element_type=F32),
            )
        )
    return found


def write_sums(z, goals, ranks, acc):
    for goal, rank in zip(goals, ranks):
        rows = pl.ds(pl.multiple_of(rank * z.tok, z.tok), z.tok)
        for h in range(z.batch):
            goal[0, :, z.lanes(h)] = (acc[h, rows, : z.width] * z.inv_root).astype(BF16)
            goal[1, :, z.lanes(h)] = acc[h, rows, z.width :].astype(BF16)


def merge_sums(parts):
    merged = []
    for h in range(len(parts[0][0])):
        peak = parts[0][0][h]
        for part in parts[1:]:
            peak = jnp.maximum(peak, part[0][h])
        fades = [jnp.exp2(part[0][h] - peak) for part in parts]
        merged.append(
            [peak] + [sum(part[i][h] * fade for part, fade in zip(parts, fades)) for i in (1, 2)]
        )
    return merged


def read_sums(stats, heads, at):
    return [[stats[h, at, i : i + 1, :] for h in heads] for i in range(3)]


def own_kernel(z, meta_ref, bias, *refs):
    full, refs = refs[: z.shards], refs[z.shards :]
    count = 3 * (z.replicas - 1)
    others, (kt, vt, both, score, dprob, stats, kv, ranked) = by_hop(z, refs[:count]), refs[count:]
    first = z.first_head(meta_ref)
    heads = range(z.batch)
    spans, ranks = z.ranks(meta_ref, False)
    order_tiles(z, full, ranks, kv, kt, vt)
    for span, rank in zip(spans, ranks):
        ranked[rank] = bias[span]
    for at, count, _ in z.queries(meta_ref, False):
        for h in heads:
            for i in range(2):
                for j in range(2):
                    ref, base = (full[at], 2) if at < z.shards else (others[at - z.shards], 0)
                    block = ref[base + i, :, z.lanes(h)]
                    both[h, at, pl.ds(i * z.tok, z.tok), z.lanes(j)] = (
                        block if i == j else jnp.zeros_like(block)
                    )
        for h in heads:
            for i in range(3):
                stats[h, at, i : i + 1, :] = jnp.full((1, z.tok), 0.0 if i else -3e38, F32)
        for rows, needed in z.blocks(count):

            @pl.when(needed)
            def _():
                sums = softmax_sums(
                    z,
                    first,
                    count,
                    rows,
                    ranked,
                    kv,
                    [both.at[h, at] for h in heads],
                    [score.at[h, at] for h in heads],
                    [dprob.at[h, at] for h in heads],
                )
                for h in heads:
                    for i in range(3):
                        stats[h, at, i : i + 1, :] = sums[i][h]


def ahead_kernel(z, meta_ref, bias, both, stats, *refs):
    tiles, (merged, kt, vt, score, dprob, kv, ranked) = by_hop(z, refs[:3]), refs[3:]
    first = z.first_head(meta_ref)
    heads = range(z.batch)
    spans, ranks = z.ranks(meta_ref, True)
    order_tiles(z, tiles, ranks, kv, kt, vt)
    for span, rank in zip(spans, ranks):
        ranked[rank] = bias[span]
    for at, count, live in z.queries(meta_ref, True):
        merged[:, at] = stats[:, at]

        for rows, needed in z.blocks(count):

            @pl.when(needed & (live == 1))
            def _():
                far = softmax_sums(
                    z,
                    first,
                    count,
                    rows,
                    ranked,
                    kv,
                    [both.at[h, at] for h in heads],
                    [score.at[h, at] for h in heads],
                    [dprob.at[h, at] for h in heads],
                )
                sums = merge_sums([read_sums(stats, heads, at), far])
                for h in heads:
                    for i in range(3):
                        merged[h, at, i : i + 1, :] = sums[h][i]


def back_kernel(z, meta_ref, both, stats, kt, vt, score, dprob, *refs):
    others, refs = refs[: z.replicas - 1], refs[z.replicas - 1 :]
    final, ot, dqt, own_sums, sums, acc = refs
    heads = range(z.batch)
    acc[...] = jnp.zeros_like(acc)
    for at, count, live in z.queries(meta_ref, True):
        parts = [read_sums(stats, heads, at)]
        for turn, other in enumerate(others, 1):
            place = (at // z.shards - turn) % z.replicas * z.shards + at % z.shards
            parts.append(read_sums(other, heads, place))
        log_total, delta = [], []
        for h, (peak, total, mixed) in enumerate(merge_sums(parts)):
            log_total.append(peak + jnp.log2(total))
            delta.append(mixed / total)
            final[h, at, 0:1, :] = log_total[h]
            final[h, at, 1:2, :] = delta[h]

        for rows, needed in z.blocks(count):

            @pl.when(needed & (live == 1))
            def _():
                found = gradients(
                    z,
                    rows,
                    log_total,
                    delta,
                    [score.at[h, at] for h in heads],
                    [dprob.at[h, at] for h in heads],
                    [both.at[h, at] for h in heads],
                    kt,
                    vt,
                    acc,
                )
                for h in heads:
                    ot[h, at], dqt[h, at] = found[h]

        @pl.when((count == 0) | (live != 1))
        def _():
            ot[:, at] = jnp.zeros_like(ot[:, at])
            dqt[:, at] = jnp.zeros_like(dqt[:, at])

    goals = [own_sums] + [sums.at[i] for i in range(z.shards - 1)]
    write_sums(z, goals, z.ranks(meta_ref, True)[1], acc)


def rows_kernel(z, meta_ref, kt, vt, both, score, dprob, final, ot_in, dqt_in, *refs, mine):
    heads = range(z.batch)
    if mine:
        acc_in, rows_out, sums, acc = refs[1], refs[2 : 2 + z.shards], refs[2 + z.shards : -1], refs[-1]
        acc[...] = acc_in[...]
    else:
        rows_out, acc = refs[1:-1], refs[-1]
        acc[...] = jnp.zeros_like(acc)
    for at, count, _ in z.queries(meta_ref, False):
        if mine != (at < z.shards):
            continue
        log_total = [final[h, at, 0:1, :] for h in heads]
        delta = [final[h, at, 1:2, :] for h in heads]

        def write(h, out, dq):
            goal = rows_out[at if mine else at - z.shards]
            goal[0, :, z.lanes(h)] = out.astype(BF16).T
            goal[1, :, z.lanes(h)] = (dq * z.inv_root).astype(BF16).T

        for rows, needed in z.blocks(count):

            @pl.when(needed)
            def _():
                found = gradients(
                    z,
                    rows,
                    log_total,
                    delta,
                    [score.at[h, at] for h in heads],
                    [dprob.at[h, at] for h in heads],
                    [both.at[h, at] for h in heads],
                    kt,
                    vt,
                    acc,
                )
                for h in heads:
                    write(h, ot_in[h, at] + found[h][0], dqt_in[h, at] + found[h][1])

        @pl.when(count == 0)
        def _():
            for h in heads:
                write(h, ot_in[h, at], dqt_in[h, at])

    if mine:
        write_sums(z, sums, z.ranks(meta_ref, False)[1], acc)


def add_up(terms, at=()):
    total = terms[0][at].astype(F32)
    for term in terms[1:]:
        total = total + term[at].astype(F32)
    return total.astype(BF16)


def add(lists):
    count = len(lists[0])

    def kernel(*refs):
        for i in range(len(lists)):
            for which in range(2):
                refs[i - len(lists)][which] = add_up(refs[i * count : (i + 1) * count], which)

    operands = [x for parts in lists for x in parts]
    return pl.pallas_call(
        kernel,
        out_shape=[jax.ShapeDtypeStruct(operands[0].shape, BF16)] * len(lists),
        in_specs=[whole(VMEM)] * len(operands),
        out_specs=[whole(VMEM)] * len(lists),
        compiler_params=params(8),
        name="add",
    )(*operands)


def merge(lists, joined, last):
    count = len(lists[0])

    def kernel(*refs):
        refs, outs = refs[: -1 - len(lists)], refs[-1 - len(lists) :]
        arrived, refs = refs[0], refs[1:]
        for which in range(2):
            for i in range(len(lists)):
                terms = list(refs[i * count : (i + 1) * count]) + [arrived.at[i]]
                outs[i][which] = add_up(terms, which)
            outs[-1][which] = add_up(refs[len(lists) * count :], which)

    operands = [joined] + [x for parts in lists for x in parts] + last
    return pl.pallas_call(
        kernel,
        out_shape=[jax.ShapeDtypeStruct(last[0].shape, BF16)] * (len(lists) + 1),
        in_specs=[whole(VMEM)] * len(operands),
        out_specs=[whole(VMEM)] * (len(lists) + 1),
        compiler_params=params(8),
        name="merge",
    )(*operands)


def unpack(pos, lists):
    shards = len(lists)
    tok, cols = lists[0][0].shape[1:]

    def kernel(pos_ref, *refs):
        ins, outs = list(refs[:-2]), refs[-2:]
        for hop in range(shards):
            terms, ins = ins[: len(lists[hop])], ins[len(lists[hop]) :]
            lanes = pl.ds(pl.multiple_of((pos_ref[0] ^ hop) * cols, 128), cols)
            for i in range(2):
                outs[i][:, lanes] = add_up(terms, i)

    operands = [x for parts in lists for x in parts]
    return pl.pallas_call(
        kernel,
        out_shape=[jax.ShapeDtypeStruct((tok, cols * shards), BF16)] * 2,
        in_specs=[whole(SMEM)] + [whole(VMEM)] * len(operands),
        out_specs=[whole(VMEM)] * 2,
        compiler_params=params(8),
        name="unpack",
    )(pos, *operands)


def per_device(queries, keys, values, grad_out, span_of_group, noise_level, next_live, level_bias):
    tok, model = queries.shape
    heads = level_bias.shape[1]
    width = model // heads
    groups = lax.axis_size("tm")
    tiles = lax.axis_size("tile")
    shards = shard_count(heads, groups)
    replicas = groups // shards
    own = heads // shards
    cols = own * width
    z = Sizes(shards, replicas, tiles, own, width, tok)
    me = lax.axis_index("tm")
    pos = jnp.stack([me // replicas, me % replicas, lax.axis_index("tile")]).astype(jnp.int32)
    meta = jnp.concatenate([pos, span_of_group, noise_level, next_live])
    shape = jax.ShapeDtypeStruct

    def to_shard(x, hop, lift):
        if hop == 0 and lift == 0:
            return x
        pairs = []
        for t in range(groups):
            goal = ((t // replicas) ^ hop) * replicas + (t - lift) % replicas
            for s in range(tiles):
                pairs.append((t * tiles + s, goal * tiles + (s + lift) % tiles))
        return lax.ppermute(x, ("tm", "tile"), pairs)

    def to_replica(x, turn):
        pairs = [(t, t // replicas * replicas + (t - turn) % replicas) for t in range(groups)]
        return lax.ppermute(x, "tm", pairs)

    def with_others(parts):
        return [
            [parts[hop]]
            + [
                to_replica(parts[turn * shards + hop], replicas - turn)
                for turn in range(1, replicas)
            ]
            for hop in hops
        ]

    def swapped(tiles):
        return [to_replica(x, turn) for turn in range(1, replicas) for x in tiles]

    hops = list(range(shards))
    last = shards - 1
    packed, (pair, early) = pack(z, pos, (keys, values, queries, grad_out))
    full = [to_shard(packed[hop], hop, 0) for hop in hops]
    far_first, far_last = to_shard(pair, 0, -1), to_shard(early, 0, -1)
    bias = bias_rows(z, meta, level_bias.T, far_first)
    direct = stack(full[1:last], 0, (far_first, far_last, bias))
    far = [far_first, to_shard(direct, 0, -1), to_shard(far_last, last, 0)]
    rows = swapped([stack(full[:1], 2, flat=True), stack(full[1:last], 2, (bias,)), stack(full[last:], 2, flat=True)])

    scalars = [(meta, "scalar")]
    one = shape((2, tok, cols), BF16)
    square = shape((own, width, shards * tok), BF16)
    block = shape((own, groups, shards * tok, tok), F32)
    stat = shape((own, groups, 8, tok), F32)
    part = shape((own, groups, width, tok), F32)
    batch = z.batch
    limit = 8 if batch == own else 56
    tiles_scratch = VMEM((batch, shards * tok, 2 * width), BF16)
    ranked_scratch = VMEM((shards, heads, tok), F32)
    sums_scratch = VMEM((batch, shards * tok, 2 * width), F32)
    kt, vt, both, score, dprob, stats = z.call(
        own_kernel,
        "own",
        limit,
        scalars + [(bias, "all")] + [(x, "lanes") for x in full + rows],
        [
            (square, "heads"),
            (square, "heads"),
            (shape((own, groups, 2 * tok, 2 * width), BF16), "heads"),
            (block, "heads"),
            (block, "heads"),
            (stat, "heads"),
        ],
        [tiles_scratch, ranked_scratch],
    )
    merged, far_kt, far_vt, far_score, far_dprob = z.call(
        ahead_kernel,
        "ahead",
        limit,
        scalars
        + [(bias, "all"), (both, "heads"), (stats, "heads")]
        + [(after(x, stats), "lanes") for x in far],
        [
            (stat, "heads"),
            (square, "heads"),
            (square, "heads"),
            (block, "heads"),
            (block, "heads"),
        ],
        [tiles_scratch, ranked_scratch],
    )
    final, ot, dqt, first_sums, far_sums = z.call(
        back_kernel,
        "back",
        limit,
        scalars
        + [(x, "heads") for x in (both, merged, far_kt, far_vt, far_score, far_dprob)]
        + [(x, "heads") for x in swapped([merged])],
        [
            (stat, "heads"),
            (part, "heads"),
            (part, "heads"),
            (one, "lanes"),
            (shape((last, 2, tok, cols), BF16), "lanes"),
        ],
        [sums_scratch],
    )
    far_home = to_shard(far_sums, 0, 1)
    operands = scalars + [(x, "heads") for x in (kt, vt, both, score, dprob, final, ot, dqt)]
    *rows_others, partial_sums = z.call(
        functools.partial(rows_kernel, mine=False),
        "rows_others",
        limit,
        operands + [(first_sums, "lanes")],
        [(one, "lanes")] * (groups - shards)
        + [(shape((own, shards * tok, 2 * width), F32), "heads")],
        [],
    )
    results = z.call(
        functools.partial(rows_kernel, mine=True),
        "rows",
        limit,
        operands + [(first_sums, "lanes"), (partial_sums, "heads")],
        [(one, "lanes")] * (2 * shards),
        [sums_scratch],
    )
    row_sums = add(with_others([*results[:shards], *rows_others]))
    rows_home = [to_shard(row_sums[hop], hop, 0) for hop in hops]
    near_sums = results[shards:]
    *sums, first_late = merge([[x] for x in near_sums[1:]], far_home, [first_sums])
    sums_home = [to_shard(x, hop, 0) for hop, x in zip(hops[1:], sums)]
    first_home = to_shard(first_late, 0, 1)
    attended, grad_queries = unpack(pos, [[x] for x in rows_home])
    grad_keys, grad_values = unpack(
        pos, [[near_sums[0], first_home]] + [[x] for x in sums_home]
    )
    return attended, grad_queries, grad_keys, grad_values


def solution(mesh):
    sharded = P(("tm", "tile"), None)
    return jax.shard_map(
        per_device,
        mesh=mesh,
        in_specs=(sharded,) * 4 + (P(),) * 4,
        out_specs=(sharded,) * 4,
        check_vma=False,
    )
```

```python
import functools
import math

import jax
import jax.numpy as jnp
from jax import lax
from jax.experimental import pallas as pl
from jax.experimental.pallas import tpu as pltpu
from jax.sharding import PartitionSpec as P

VMEM = pltpu.VMEM
SMEM = pltpu.SMEM
BF16 = jnp.bfloat16
F32 = jnp.float32
NT = (((1,), (1,)), ((), ()))
LOG2E = 1.4426950408889634
DEAD = -1e30


def params(mib):
    return pltpu.CompilerParams(vmem_limit_bytes=mib * 1024 * 1024)


def whole(space):
    return pl.BlockSpec(memory_space=space)


def shard_count(heads, groups):
    count = 1
    while heads % (2 * count) == 0 and groups % (2 * count) == 0:
        count *= 2
    return count


def fold(op, x):
    return op(x.reshape(x.shape[0] // 8, 8, x.shape[1]), axis=0)


def pack_kernel(z, pos_ref, *refs):
    sources, refs = refs[:4], refs[4:]
    outs, (pair, early, held, sems) = refs[: z.shards], refs[z.shards :]
    half, cols = z.tok // 2, z.own_heads * z.width
    copies = []
    for i, src in enumerate(sources):
        for j in range(2):
            rows = pl.ds(j * half, half)
            copy = pltpu.make_async_copy(src.at[rows], held.at[i, rows], sems.at[i, j])
            copy.start()
            copies.append(copy)
    for i in range(4):
        copies[2 * i].wait()
        copies[2 * i + 1].wait()
        for hop in range(z.shards):
            lanes = pl.ds(pl.multiple_of((pos_ref[0] ^ hop) * cols, 128), cols)
            part = held[i, :, lanes]
            outs[hop][i] = part
            if hop == 0 and i < 2:
                pair[i] = part
            if hop == z.shards - 1 and i < 2:
                early[i] = part


def pack(z, pos, arrays):
    cols = z.own_heads * z.width
    sources = [pltpu.with_memory_space_constraint(x, pltpu.HBM) for x in arrays]
    shape = jax.ShapeDtypeStruct
    results = pl.pallas_call(
        functools.partial(pack_kernel, z),
        out_shape=[shape((4, z.tok, cols), BF16)] * z.shards
        + [shape((2, z.tok, cols), BF16)] * 2,
        in_specs=[whole(SMEM)] + [whole(pltpu.HBM)] * 4,
        out_specs=[whole(VMEM)] * (z.shards + 2),
        scratch_shapes=[
            VMEM((4, z.tok, cols * z.shards), BF16),
            pltpu.SemaphoreType.DMA((4, 2)),
        ],
        compiler_params=params(8),
        name="pack",
    )(pos, *sources)
    return results[:-2], results[-2:]


def bias_kernel(z, meta_ref, table_ref, after_ref, bias):
    level_ids = lax.broadcasted_iota(jnp.int32, table_ref.shape, 1)
    for span in range(z.groups):
        column = jnp.sum(
            jnp.where(level_ids == z.level(meta_ref, span), table_ref[...], 0.0),
            axis=1,
            keepdims=True,
        )
        bias[span] = jnp.broadcast_to(column * LOG2E, bias.shape[1:])


def bias_rows(z, meta, table, other):
    return pl.pallas_call(
        functools.partial(bias_kernel, z),
        out_shape=jax.ShapeDtypeStruct((z.groups, table.shape[0], z.tok), F32),
        in_specs=[whole(SMEM), whole(VMEM), whole(pl.ANY)],
        out_specs=whole(VMEM),
        compiler_params=params(8),
        name="bias",
    )(meta, table, other)


def stack_kernel(count, base, *refs):
    out = refs[-1]
    for i in range(count):
        for j in range(2):
            if len(out.shape) == 4:
                out[i, j] = refs[i][base + j]
            else:
                out[j] = refs[i][base + j]


def stack(parts, base, others=(), flat=False):
    one = (2,) + parts[0].shape[1:]
    return pl.pallas_call(
        functools.partial(stack_kernel, len(parts), base),
        out_shape=jax.ShapeDtypeStruct(one if flat else (len(parts),) + one, BF16),
        in_specs=[whole(VMEM)] * len(parts) + [whole(pl.ANY)] * len(others),
        out_specs=whole(VMEM),
        compiler_params=params(8),
        name="stack",
    )(*parts, *others)


def after_kernel(*refs):
    pass


def after(x, *others):
    return pl.pallas_call(
        after_kernel,
        out_shape=jax.ShapeDtypeStruct(x.shape, x.dtype),
        in_specs=[whole(pl.ANY)] * (1 + len(others)),
        out_specs=whole(pl.ANY),
        input_output_aliases={0: 0},
        compiler_params=params(1),
        name="after",
    )(x, *others)


class Sizes:
    def __init__(self, shards, replicas, tiles, own_heads, width, tok):
        self.shards, self.replicas, self.tiles = shards, replicas, tiles
        self.own_heads, self.width, self.tok = own_heads, width, tok
        self.groups = shards * replicas
        self.batch = own_heads if self.groups <= 8 else 1
        self.inv_root = 1.0 / math.sqrt(width)

    def group_of(self, meta_ref, turn, hop):
        return (meta_ref[0] ^ hop) * self.replicas + lax.rem(meta_ref[1] + turn, self.replicas)

    def span(self, meta_ref, turn, hop):
        return meta_ref[3 + self.group_of(meta_ref, turn, hop)]

    def level(self, meta_ref, span):
        return meta_ref[3 + self.groups + span]

    def live(self, meta_ref, turn, hop):
        tile = self.group_of(meta_ref, turn, hop) * self.tiles + meta_ref[2]
        return meta_ref[3 + 2 * self.groups + tile]

    def ranks(self, meta_ref, ahead):
        turn = self.replicas - 1 if ahead else 0
        spans = [self.span(meta_ref, turn, hop) for hop in range(self.shards)]
        return spans, [sum(jnp.where(x < span, 1, 0) for x in spans) for span in spans]

    def queries(self, meta_ref, ahead):
        spans, _ = self.ranks(meta_ref, ahead)
        for turn in range(self.replicas):
            for hop in range(self.shards):
                span = self.span(meta_ref, turn, hop)
                count = sum(jnp.where(x <= span, 1, 0) for x in spans)
                yield turn * self.shards + hop, count, self.live(meta_ref, turn, hop)

    def lanes(self, h):
        return pl.ds(h * self.width, self.width)

    def first_head(self, meta_ref):
        base = 0 if self.batch == self.own_heads else pl.program_id(0) * self.batch
        return meta_ref[0] * self.own_heads + base

    def blocks(self, count):
        for steps in range(1, self.shards // 2 + 1):
            yield 2 * steps * self.tok, lax.div(count + 1, 2) == steps

    def call(self, kernel, name, limit, operands, outs, scratch):
        split = self.batch != self.own_heads

        def spec(shape, kind):
            if kind == "scalar":
                return whole(SMEM)
            if not split:
                return whole(VMEM)
            block, axis = list(shape), {"heads": 0, "lanes": len(shape) - 1}.get(kind)
            if axis is None:
                return pl.BlockSpec(tuple(block), lambda h: (0,) * len(block))
            block[axis] = block[axis] // self.own_heads * self.batch
            return pl.BlockSpec(
                tuple(block), lambda h: tuple(h if d == axis else 0 for d in range(len(block)))
            )

        return pl.pallas_call(
            functools.partial(kernel, self),
            grid=(self.own_heads // self.batch,) if split else (),
            in_specs=[spec(x.shape, kind) for x, kind in operands],
            out_specs=[spec(x.shape, kind) for x, kind in outs],
            out_shape=[x for x, kind in outs],
            scratch_shapes=scratch,
            compiler_params=params(limit),
            name=name,
        )(*(x for x, kind in operands))


def by_hop(z, refs):
    found = []
    for turn in range(len(refs) // 3):
        first, middle, last = refs[3 * turn : 3 * turn + 3]
        found += [first] + [middle.at[i] for i in range(z.shards - 2)] + [last]
    return found


def order_tiles(z, tiles, ranks, kv, kt, vt):
    for ref, rank in zip(tiles, ranks):
        rows = pl.ds(pl.multiple_of(rank * z.tok, z.tok), z.tok)
        for h in range(z.batch):
            k, v = ref[0, :, z.lanes(h)], ref[1, :, z.lanes(h)]
            kv[h, rows, : z.width] = k
            kv[h, rows, z.width :] = v
            kt[h, :, rows] = k.T
            vt[h, :, rows] = v.T


def softmax_sums(z, first, count, rows, bias, kv, both, score, dprob):
    scale = z.inv_root * LOG2E
    sums = []
    for h in range(z.batch):
        sd = lax.dot_general(kv[h, :rows, :], both[h][...], NT, preferred_element_type=F32)
        parts = []
        for rank in range(rows // z.tok):
            shift = bias[rank, pl.ds(first + h, 1), :] + jnp.where(rank < count, 0.0, DEAD)
            parts.append(sd[rank * z.tok : (rank + 1) * z.tok, : z.tok] * scale + shift)
        s, dp = jnp.concatenate(parts, axis=0), sd[:, z.tok :]
        score[h][:rows, :] = s
        dprob[h][:rows, :] = dp
        peak = jnp.max(fold(jnp.max, s), axis=0, keepdims=True)
        e = jnp.exp2(s - peak)
        total = jnp.sum(fold(jnp.sum, e), axis=0, keepdims=True)
        mixed = jnp.sum(fold(jnp.sum, e * dp), axis=0, keepdims=True)
        sums.append((peak, total, mixed))
    return [[x[i] for x in sums] for i in range(3)]


def weights(z, rows, log_total, delta, score, dprob):
    for h in range(z.batch):
        w = jnp.exp2(score[h][:rows, :] - log_total[h])
        yield h, w.astype(BF16), (w * (dprob[h][:rows, :] - delta[h])).astype(BF16)


def add_key_gradients(rows, pairs, both, acc):
    for h, w, ds in pairs:
        acc[h, :rows, :] += jnp.dot(
            jnp.concatenate([ds, w], axis=1), both[h][...], preferred_element_type=F32
        )


def row_gradients(rows, pairs, kt, vt):
    return [
        (
            jnp.dot(vt[h, :, :rows], w, preferred_element_type=F32),
            jnp.dot(kt[h, :, :rows], ds, preferred_element_type=F32),
        )
        for h, w, ds in pairs
    ]


def write_sums(z, goals, ranks, acc):
    for goal, rank in zip(goals, ranks):
        rows = pl.ds(pl.multiple_of(rank * z.tok, z.tok), z.tok)
        for h in range(z.batch):
            goal[0, :, z.lanes(h)] = (acc[h, rows, : z.width] * z.inv_root).astype(BF16)
            goal[1, :, z.lanes(h)] = acc[h, rows, z.width :].astype(BF16)


def merge_sums(parts):
    merged = []
    for h in range(len(parts[0][0])):
        peak = parts[0][0][h]
        for part in parts[1:]:
            peak = jnp.maximum(peak, part[0][h])
        fades = [jnp.exp2(part[0][h] - peak) for part in parts]
        merged.append(
            [peak] + [sum(part[i][h] * fade for part, fade in zip(parts, fades)) for i in (1, 2)]
        )
    return merged


def read_sums(stats, heads, at):
    return [[stats[h, at, i : i + 1, :] for h in heads] for i in range(3)]


def own_kernel(z, meta_ref, bias, *refs):
    full, refs = refs[: z.shards], refs[z.shards :]
    count = 3 * (z.replicas - 1)
    others, (kt, vt, both, score, dprob, stats, kv, ranked) = by_hop(z, refs[:count]), refs[count:]
    first = z.first_head(meta_ref)
    heads = range(z.batch)
    spans, ranks = z.ranks(meta_ref, False)
    order_tiles(z, full, ranks, kv, kt, vt)
    for span, rank in zip(spans, ranks):
        ranked[rank] = bias[span]
    for at, count, _ in z.queries(meta_ref, False):
        for h in heads:
            for i in range(2):
                for j in range(2):
                    ref, base = (full[at], 2) if at < z.shards else (others[at - z.shards], 0)
                    block = ref[base + i, :, z.lanes(h)]
                    both[h, at, pl.ds(i * z.tok, z.tok), z.lanes(j)] = (
                        block if i == j else jnp.zeros_like(block)
                    )
        for h in heads:
            for i in range(3):
                stats[h, at, i : i + 1, :] = jnp.full((1, z.tok), 0.0 if i else -3e38, F32)
        for rows, needed in z.blocks(count):

            @pl.when(needed)
            def _():
                sums = softmax_sums(
                    z,
                    first,
                    count,
                    rows,
                    ranked,
                    kv,
                    [both.at[h, at] for h in heads],
                    [score.at[h, at] for h in heads],
                    [dprob.at[h, at] for h in heads],
                )
                for h in heads:
                    for i in range(3):
                        stats[h, at, i : i + 1, :] = sums[i][h]


def ahead_kernel(z, meta_ref, bias, both, stats, *refs):
    tiles, (merged, kt, vt, score, dprob, kv, ranked) = by_hop(z, refs[:3]), refs[3:]
    first = z.first_head(meta_ref)
    heads = range(z.batch)
    spans, ranks = z.ranks(meta_ref, True)
    order_tiles(z, tiles, ranks, kv, kt, vt)
    for span, rank in zip(spans, ranks):
        ranked[rank] = bias[span]
    for at, count, live in z.queries(meta_ref, True):
        merged[:, at] = stats[:, at]

        for rows, needed in z.blocks(count):

            @pl.when(needed & (live == 1))
            def _():
                far = softmax_sums(
                    z,
                    first,
                    count,
                    rows,
                    ranked,
                    kv,
                    [both.at[h, at] for h in heads],
                    [score.at[h, at] for h in heads],
                    [dprob.at[h, at] for h in heads],
                )
                sums = merge_sums([read_sums(stats, heads, at), far])
                for h in heads:
                    for i in range(3):
                        merged[h, at, i : i + 1, :] = sums[h][i]


def back_kernel(z, meta_ref, both, stats, kt, vt, score, dprob, *refs):
    others, refs = refs[: z.replicas - 1], refs[z.replicas - 1 :]
    final, ot, dqt, own_sums, sums, acc = refs
    heads = range(z.batch)
    acc[...] = jnp.zeros_like(acc)
    for at, count, live in z.queries(meta_ref, True):
        parts = [read_sums(stats, heads, at)]
        for turn, other in enumerate(others, 1):
            place = (at // z.shards - turn) % z.replicas * z.shards + at % z.shards
            parts.append(read_sums(other, heads, place))
        log_total, delta = [], []
        for h, (peak, total, mixed) in enumerate(merge_sums(parts)):
            log_total.append(peak + jnp.log2(total))
            delta.append(mixed / total)
            final[h, at, 0:1, :] = log_total[h]
            final[h, at, 1:2, :] = delta[h]

        for rows, needed in z.blocks(count):

            @pl.when(needed & (live == 1))
            def _():
                pairs = list(
                    weights(
                        z,
                        rows,
                        log_total,
                        delta,
                        [score.at[h, at] for h in heads],
                        [dprob.at[h, at] for h in heads],
                    )
                )
                add_key_gradients(rows, pairs, [both.at[h, at] for h in heads], acc)
                for h, found in enumerate(row_gradients(rows, pairs, kt, vt)):
                    ot[h, at], dqt[h, at] = found

        @pl.when((count == 0) | (live != 1))
        def _():
            ot[:, at] = jnp.zeros_like(ot[:, at])
            dqt[:, at] = jnp.zeros_like(dqt[:, at])

    goals = [own_sums] + [sums.at[i] for i in range(z.shards - 1)]
    write_sums(z, goals, z.ranks(meta_ref, True)[1], acc)


def rows_kernel(z, meta_ref, kt, vt, score, dprob, final, ot_in, dqt_in, *refs, mine):
    rows_out = refs[1:]
    heads = range(z.batch)
    for at, count, _ in z.queries(meta_ref, False):
        if mine != (at < z.shards):
            continue
        log_total = [final[h, at, 0:1, :] for h in heads]
        delta = [final[h, at, 1:2, :] for h in heads]

        def write(h, out, dq):
            goal = rows_out[at if mine else at - z.shards]
            goal[0, :, z.lanes(h)] = out.astype(BF16).T
            goal[1, :, z.lanes(h)] = (dq * z.inv_root).astype(BF16).T

        for rows, needed in z.blocks(count):

            @pl.when(needed)
            def _():
                pairs = weights(
                    z,
                    rows,
                    log_total,
                    delta,
                    [score.at[h, at] for h in heads],
                    [dprob.at[h, at] for h in heads],
                )
                for h, (out, dq) in enumerate(row_gradients(rows, pairs, kt, vt)):
                    write(h, ot_in[h, at] + out, dqt_in[h, at] + dq)

        @pl.when(count == 0)
        def _():
            for h in heads:
                write(h, ot_in[h, at], dqt_in[h, at])


def sums_kernel(z, meta_ref, both, score, dprob, final, *refs):
    sums, acc = refs[1:-1], refs[-1]
    heads = range(z.batch)
    acc[...] = jnp.zeros_like(acc)
    for at, count, _ in z.queries(meta_ref, False):
        for rows, needed in z.blocks(count):

            @pl.when(needed)
            def _():
                pairs = weights(
                    z,
                    rows,
                    [final[h, at, 0:1, :] for h in heads],
                    [final[h, at, 1:2, :] for h in heads],
                    [score.at[h, at] for h in heads],
                    [dprob.at[h, at] for h in heads],
                )
                add_key_gradients(rows, pairs, [both.at[h, at] for h in heads], acc)

    write_sums(z, sums, z.ranks(meta_ref, False)[1], acc)


def add_up(terms, at=()):
    total = terms[0][at].astype(F32)
    for term in terms[1:]:
        total = total + term[at].astype(F32)
    return total.astype(BF16)


def add(lists):
    count = len(lists[0])

    def kernel(*refs):
        for i in range(len(lists)):
            for which in range(2):
                refs[i - len(lists)][which] = add_up(refs[i * count : (i + 1) * count], which)

    operands = [x for parts in lists for x in parts]
    return pl.pallas_call(
        kernel,
        out_shape=[jax.ShapeDtypeStruct(operands[0].shape, BF16)] * len(lists),
        in_specs=[whole(VMEM)] * len(operands),
        out_specs=[whole(VMEM)] * len(lists),
        compiler_params=params(8),
        name="add",
    )(*operands)


def merge(lists, joined, last):
    count = len(lists[0])

    def kernel(*refs):
        refs, outs = refs[: -1 - len(lists)], refs[-1 - len(lists) :]
        arrived, refs = refs[0], refs[1:]
        for which in range(2):
            for i in range(len(lists)):
                terms = list(refs[i * count : (i + 1) * count]) + [arrived.at[i]]
                outs[i][which] = add_up(terms, which)
            outs[-1][which] = add_up(refs[len(lists) * count :], which)

    operands = [joined] + [x for parts in lists for x in parts] + last
    return pl.pallas_call(
        kernel,
        out_shape=[jax.ShapeDtypeStruct(last[0].shape, BF16)] * (len(lists) + 1),
        in_specs=[whole(VMEM)] * len(operands),
        out_specs=[whole(VMEM)] * (len(lists) + 1),
        compiler_params=params(8),
        name="merge",
    )(*operands)


def unpack(pos, lists):
    shards = len(lists)
    tok, cols = lists[0][0].shape[1:]

    def kernel(pos_ref, *refs):
        ins, outs = list(refs[:-2]), refs[-2:]
        for hop in range(shards):
            terms, ins = ins[: len(lists[hop])], ins[len(lists[hop]) :]
            lanes = pl.ds(pl.multiple_of((pos_ref[0] ^ hop) * cols, 128), cols)
            for i in range(2):
                outs[i][:, lanes] = add_up(terms, i)

    operands = [x for parts in lists for x in parts]
    return pl.pallas_call(
        kernel,
        out_shape=[jax.ShapeDtypeStruct((tok, cols * shards), BF16)] * 2,
        in_specs=[whole(SMEM)] + [whole(VMEM)] * len(operands),
        out_specs=[whole(VMEM)] * 2,
        compiler_params=params(8),
        name="unpack",
    )(pos, *operands)


def per_device(queries, keys, values, grad_out, span_of_group, noise_level, next_live, level_bias):
    tok, model = queries.shape
    heads = level_bias.shape[1]
    width = model // heads
    groups = lax.axis_size("tm")
    tiles = lax.axis_size("tile")
    shards = shard_count(heads, groups)
    replicas = groups // shards
    own = heads // shards
    cols = own * width
    z = Sizes(shards, replicas, tiles, own, width, tok)
    me = lax.axis_index("tm")
    pos = jnp.stack([me // replicas, me % replicas, lax.axis_index("tile")]).astype(jnp.int32)
    meta = jnp.concatenate([pos, span_of_group, noise_level, next_live])
    shape = jax.ShapeDtypeStruct

    def to_shard(x, hop, lift):
        if hop == 0 and lift == 0:
            return x
        pairs = []
        for t in range(groups):
            goal = ((t // replicas) ^ hop) * replicas + (t - lift) % replicas
            for s in range(tiles):
                pairs.append((t * tiles + s, goal * tiles + (s + lift) % tiles))
        return lax.ppermute(x, ("tm", "tile"), pairs)

    def to_replica(x, turn):
        pairs = [(t, t // replicas * replicas + (t - turn) % replicas) for t in range(groups)]
        return lax.ppermute(x, "tm", pairs)

    def with_others(parts):
        return [
            [parts[hop]]
            + [
                to_replica(parts[turn * shards + hop], replicas - turn)
                for turn in range(1, replicas)
            ]
            for hop in hops
        ]

    def swapped(tiles):
        return [to_replica(x, turn) for turn in range(1, replicas) for x in tiles]

    hops = list(range(shards))
    last = shards - 1
    packed, (pair, early) = pack(z, pos, (keys, values, queries, grad_out))
    full = [to_shard(packed[hop], hop, 0) for hop in hops]
    far_first, far_last = to_shard(pair, 0, -1), to_shard(early, 0, -1)
    bias = bias_rows(z, meta, level_bias.T, far_first)
    direct = stack(full[1:last], 0, (far_first, far_last, bias))
    far = [far_first, to_shard(direct, 0, -1), to_shard(far_last, last, 0)]
    rows = swapped([stack(full[:1], 2, flat=True), stack(full[1:last], 2, (bias,)), stack(full[last:], 2, flat=True)])

    scalars = [(meta, "scalar")]
    one = shape((2, tok, cols), BF16)
    square = shape((own, width, shards * tok), BF16)
    block = shape((own, groups, shards * tok, tok), F32)
    stat = shape((own, groups, 8, tok), F32)
    part = shape((own, groups, width, tok), F32)
    batch = z.batch
    limit = 8 if batch == own else 56
    tiles_scratch = VMEM((batch, shards * tok, 2 * width), BF16)
    ranked_scratch = VMEM((shards, heads, tok), F32)
    sums_scratch = VMEM((batch, shards * tok, 2 * width), F32)
    kt, vt, both, score, dprob, stats = z.call(
        own_kernel,
        "own",
        limit,
        scalars + [(bias, "all")] + [(x, "lanes") for x in full + rows],
        [
            (square, "heads"),
            (square, "heads"),
            (shape((own, groups, 2 * tok, 2 * width), BF16), "heads"),
            (block, "heads"),
            (block, "heads"),
            (stat, "heads"),
        ],
        [tiles_scratch, ranked_scratch],
    )
    merged, far_kt, far_vt, far_score, far_dprob = z.call(
        ahead_kernel,
        "ahead",
        limit,
        scalars
        + [(bias, "all"), (both, "heads"), (stats, "heads")]
        + [(after(x, stats), "lanes") for x in far],
        [
            (stat, "heads"),
            (square, "heads"),
            (square, "heads"),
            (block, "heads"),
            (block, "heads"),
        ],
        [tiles_scratch, ranked_scratch],
    )
    final, ot, dqt, first_sums, far_sums = z.call(
        back_kernel,
        "back",
        limit,
        scalars
        + [(x, "heads") for x in (both, merged, far_kt, far_vt, far_score, far_dprob)]
        + [(x, "heads") for x in swapped([merged])],
        [
            (stat, "heads"),
            (part, "heads"),
            (part, "heads"),
            (one, "lanes"),
            (shape((last, 2, tok, cols), BF16), "lanes"),
        ],
        [sums_scratch],
    )
    far_home = to_shard(far_sums, 0, 1)
    operands = scalars + [(x, "heads") for x in (kt, vt, score, dprob, final, ot, dqt)]
    rows_others = z.call(
        functools.partial(rows_kernel, mine=False),
        "rows_others",
        limit,
        operands + [(first_sums, "lanes")],
        [(one, "lanes")] * (groups - shards),
        [],
    )
    rows_mine = z.call(
        functools.partial(rows_kernel, mine=True),
        "rows",
        limit,
        operands + [(first_sums, "lanes")],
        [(one, "lanes")] * shards,
        [],
    )
    row_sums = add(with_others([*rows_mine, *rows_others]))
    rows_home = [to_shard(row_sums[hop], hop, 0) for hop in hops[::-1]][::-1]
    near_sums = z.call(
        sums_kernel,
        "sums",
        limit,
        scalars
        + [(x, "heads") for x in (both, score, dprob, final)]
        + [(row_sums[0], "lanes")],
        [(one, "lanes")] * shards,
        [sums_scratch],
    )
    *sums, first_late = merge([[x] for x in near_sums[1:]], far_home, [first_sums])
    sums_home = [to_shard(x, hop, 0) for hop, x in zip(hops[:0:-1], sums[::-1])][::-1]
    first_home = to_shard(first_late, 0, 1)
    attended, grad_queries = unpack(pos, [[x] for x in rows_home])
    grad_keys, grad_values = unpack(
        pos, [[near_sums[0], first_home]] + [[x] for x in sums_home]
    )
    return attended, grad_queries, grad_keys, grad_values


def solution(mesh):
    sharded = P(("tm", "tile"), None)
    return jax.shard_map(
        per_device,
        mesh=mesh,
        in_specs=(sharded,) * 4 + (P(),) * 4,
        out_specs=(sharded,) * 4,
        check_vma=False,
    )
```

```python
import functools
import math

import jax
import jax.numpy as jnp
from jax import lax
from jax.experimental import pallas as pl
from jax.experimental.pallas import tpu as pltpu
from jax.sharding import PartitionSpec as P

VMEM = pltpu.VMEM
SMEM = pltpu.SMEM
BF16 = jnp.bfloat16
F32 = jnp.float32
NT = (((1,), (1,)), ((), ()))
LOG2E = 1.4426950408889634
DEAD = -1e30


def params(mib):
    return pltpu.CompilerParams(vmem_limit_bytes=mib * 1024 * 1024)


def whole(space):
    return pl.BlockSpec(memory_space=space)


def shard_count(heads, groups):
    count = 1
    while heads % (2 * count) == 0 and groups % (2 * count) == 0:
        count *= 2
    return count


def fold(op, x):
    return op(x.reshape(x.shape[0] // 8, 8, x.shape[1]), axis=0)


def pack_kernel(z, pos_ref, *refs):
    sources, refs = refs[:4], refs[4:]
    outs, (pair, early, held, sems) = refs[: z.shards], refs[z.shards :]
    half, cols = z.tok // 2, z.own_heads * z.width
    copies = []
    for i, src in enumerate(sources):
        for j in range(2):
            rows = pl.ds(j * half, half)
            copy = pltpu.make_async_copy(src.at[rows], held.at[i, rows], sems.at[i, j])
            copy.start()
            copies.append(copy)
    for i in range(4):
        copies[2 * i].wait()
        copies[2 * i + 1].wait()
        for hop in range(z.shards):
            lanes = pl.ds(pl.multiple_of((pos_ref[0] ^ hop) * cols, 128), cols)
            part = held[i, :, lanes]
            outs[hop][i] = part
            if hop == 0 and i < 2:
                pair[i] = part
            if hop == z.shards - 1 and i < 2:
                early[i] = part


def pack(z, pos, arrays):
    cols = z.own_heads * z.width
    sources = [pltpu.with_memory_space_constraint(x, pltpu.HBM) for x in arrays]
    shape = jax.ShapeDtypeStruct
    results = pl.pallas_call(
        functools.partial(pack_kernel, z),
        out_shape=[shape((4, z.tok, cols), BF16)] * z.shards
        + [shape((2, z.tok, cols), BF16)] * 2,
        in_specs=[whole(SMEM)] + [whole(pltpu.HBM)] * 4,
        out_specs=[whole(VMEM)] * (z.shards + 2),
        scratch_shapes=[
            VMEM((4, z.tok, cols * z.shards), BF16),
            pltpu.SemaphoreType.DMA((4, 2)),
        ],
        compiler_params=params(8),
        name="pack",
    )(pos, *sources)
    return results[:-2], results[-2:]


def bias_kernel(z, meta_ref, table_ref, after_ref, bias):
    level_ids = lax.broadcasted_iota(jnp.int32, table_ref.shape, 1)
    for span in range(z.groups):
        column = jnp.sum(
            jnp.where(level_ids == z.level(meta_ref, span), table_ref[...], 0.0),
            axis=1,
            keepdims=True,
        )
        bias[span] = jnp.broadcast_to(column * LOG2E, bias.shape[1:])


def bias_rows(z, meta, table, other):
    return pl.pallas_call(
        functools.partial(bias_kernel, z),
        out_shape=jax.ShapeDtypeStruct((z.groups, table.shape[0], z.tok), F32),
        in_specs=[whole(SMEM), whole(VMEM), whole(pl.ANY)],
        out_specs=whole(VMEM),
        compiler_params=params(8),
        name="bias",
    )(meta, table, other)


def stack_kernel(count, base, *refs):
    out = refs[-1]
    for i in range(count):
        for j in range(2):
            if len(out.shape) == 4:
                out[i, j] = refs[i][base + j]
            else:
                out[j] = refs[i][base + j]


def stack(parts, base, others=(), flat=False):
    one = (2,) + parts[0].shape[1:]
    return pl.pallas_call(
        functools.partial(stack_kernel, len(parts), base),
        out_shape=jax.ShapeDtypeStruct(one if flat else (len(parts),) + one, BF16),
        in_specs=[whole(VMEM)] * len(parts) + [whole(pl.ANY)] * len(others),
        out_specs=whole(VMEM),
        compiler_params=params(8),
        name="stack",
    )(*parts, *others)


def after_kernel(*refs):
    pass


def after(x, *others):
    return pl.pallas_call(
        after_kernel,
        out_shape=jax.ShapeDtypeStruct(x.shape, x.dtype),
        in_specs=[whole(pl.ANY)] * (1 + len(others)),
        out_specs=whole(pl.ANY),
        input_output_aliases={0: 0},
        compiler_params=params(1),
        name="after",
    )(x, *others)


class Sizes:
    def __init__(self, shards, replicas, tiles, own_heads, width, tok):
        self.shards, self.replicas, self.tiles = shards, replicas, tiles
        self.own_heads, self.width, self.tok = own_heads, width, tok
        self.groups = shards * replicas
        self.batch = own_heads if self.groups <= 8 else 1
        self.inv_root = 1.0 / math.sqrt(width)

    def group_of(self, meta_ref, turn, hop):
        return (meta_ref[0] ^ hop) * self.replicas + lax.rem(meta_ref[1] + turn, self.replicas)

    def span(self, meta_ref, turn, hop):
        return meta_ref[3 + self.group_of(meta_ref, turn, hop)]

    def level(self, meta_ref, span):
        return meta_ref[3 + self.groups + span]

    def live(self, meta_ref, turn, hop):
        tile = self.group_of(meta_ref, turn, hop) * self.tiles + meta_ref[2]
        return meta_ref[3 + 2 * self.groups + tile]

    def ranks(self, meta_ref, ahead):
        turn = self.replicas - 1 if ahead else 0
        spans = [self.span(meta_ref, turn, hop) for hop in range(self.shards)]
        return spans, [sum(jnp.where(x < span, 1, 0) for x in spans) for span in spans]

    def queries(self, meta_ref, ahead):
        spans, _ = self.ranks(meta_ref, ahead)
        for turn in range(self.replicas):
            for hop in range(self.shards):
                span = self.span(meta_ref, turn, hop)
                count = sum(jnp.where(x <= span, 1, 0) for x in spans)
                yield turn * self.shards + hop, count, self.live(meta_ref, turn, hop)

    def lanes(self, h):
        return pl.ds(h * self.width, self.width)

    def first_head(self, meta_ref):
        base = 0 if self.batch == self.own_heads else pl.program_id(0) * self.batch
        return meta_ref[0] * self.own_heads + base

    def blocks(self, count):
        for steps in range(1, self.shards // 2 + 1):
            yield 2 * steps * self.tok, lax.div(count + 1, 2) == steps

    def call(self, kernel, name, limit, operands, outs, scratch):
        split = self.batch != self.own_heads

        def spec(shape, kind):
            if kind == "scalar":
                return whole(SMEM)
            if not split:
                return whole(VMEM)
            block, axis = list(shape), {"heads": 0, "lanes": len(shape) - 1}.get(kind)
            if axis is None:
                return pl.BlockSpec(tuple(block), lambda h: (0,) * len(block))
            block[axis] = block[axis] // self.own_heads * self.batch
            return pl.BlockSpec(
                tuple(block), lambda h: tuple(h if d == axis else 0 for d in range(len(block)))
            )

        return pl.pallas_call(
            functools.partial(kernel, self),
            grid=(self.own_heads // self.batch,) if split else (),
            in_specs=[spec(x.shape, kind) for x, kind in operands],
            out_specs=[spec(x.shape, kind) for x, kind in outs],
            out_shape=[x for x, kind in outs],
            scratch_shapes=scratch,
            compiler_params=params(limit),
            name=name,
        )(*(x for x, kind in operands))


def by_hop(z, refs):
    found = []
    for turn in range(len(refs) // 3):
        first, middle, last = refs[3 * turn : 3 * turn + 3]
        found += [first] + [middle.at[i] for i in range(z.shards - 2)] + [last]
    return found


def order_tiles(z, tiles, ranks, kv, kt, vt):
    for ref, rank in zip(tiles, ranks):
        rows = pl.ds(pl.multiple_of(rank * z.tok, z.tok), z.tok)
        for h in range(z.batch):
            k, v = ref[0, :, z.lanes(h)], ref[1, :, z.lanes(h)]
            kv[h, rows, : z.width] = k
            kv[h, rows, z.width :] = v
            kt[h, :, rows] = k.T
            vt[h, :, rows] = v.T


def softmax_sums(z, first, count, rows, bias, kv, both, score, dprob):
    scale = z.inv_root * LOG2E
    sums = []
    for h in range(z.batch):
        sd = lax.dot_general(kv[h, :rows, :], both[h][...], NT, preferred_element_type=F32)
        parts = []
        for rank in range(rows // z.tok):
            shift = bias[rank, pl.ds(first + h, 1), :] + jnp.where(rank < count, 0.0, DEAD)
            parts.append(sd[rank * z.tok : (rank + 1) * z.tok, : z.tok] * scale + shift)
        s, dp = jnp.concatenate(parts, axis=0), sd[:, z.tok :]
        score[h][:rows, :] = s
        dprob[h][:rows, :] = dp
        peak = jnp.max(fold(jnp.max, s), axis=0, keepdims=True)
        e = jnp.exp2(s - peak)
        total = jnp.sum(fold(jnp.sum, e), axis=0, keepdims=True)
        mixed = jnp.sum(fold(jnp.sum, e * dp), axis=0, keepdims=True)
        sums.append((peak, total, mixed))
    return [[x[i] for x in sums] for i in range(3)]


def weights(z, rows, log_total, delta, score, dprob):
    for h in range(z.batch):
        w = jnp.exp2(score[h][:rows, :] - log_total[h])
        yield h, w.astype(BF16), (w * (dprob[h][:rows, :] - delta[h])).astype(BF16)


def add_key_gradients(rows, pairs, both, acc):
    for h, w, ds in pairs:
        acc[h, :rows, :] += jnp.dot(
            jnp.concatenate([ds, w], axis=1), both[h][...], preferred_element_type=F32
        )


def row_gradients(rows, pairs, kt, vt):
    return [
        (
            jnp.dot(vt[h, :, :rows], w, preferred_element_type=F32),
            jnp.dot(kt[h, :, :rows], ds, preferred_element_type=F32),
        )
        for h, w, ds in pairs
    ]


def write_sums(z, goals, ranks, acc):
    for goal, rank in zip(goals, ranks):
        rows = pl.ds(pl.multiple_of(rank * z.tok, z.tok), z.tok)
        for h in range(z.batch):
            goal[0, :, z.lanes(h)] = (acc[h, rows, : z.width] * z.inv_root).astype(BF16)
            goal[1, :, z.lanes(h)] = acc[h, rows, z.width :].astype(BF16)


def merge_sums(parts):
    merged = []
    for h in range(len(parts[0][0])):
        peak = parts[0][0][h]
        for part in parts[1:]:
            peak = jnp.maximum(peak, part[0][h])
        fades = [jnp.exp2(part[0][h] - peak) for part in parts]
        merged.append(
            [peak] + [sum(part[i][h] * fade for part, fade in zip(parts, fades)) for i in (1, 2)]
        )
    return merged


def read_sums(stats, heads, at):
    return [[stats[h, at, i : i + 1, :] for h in heads] for i in range(3)]


def own_kernel(z, meta_ref, bias, *refs):
    full, refs = refs[: z.shards], refs[z.shards :]
    count = 3 * (z.replicas - 1)
    others, (kt, vt, both, score, dprob, stats, kv, ranked) = by_hop(z, refs[:count]), refs[count:]
    first = z.first_head(meta_ref)
    heads = range(z.batch)
    spans, ranks = z.ranks(meta_ref, False)
    order_tiles(z, full, ranks, kv, kt, vt)
    for span, rank in zip(spans, ranks):
        ranked[rank] = bias[span]
    for at, count, _ in z.queries(meta_ref, False):
        for h in heads:
            for i in range(2):
                for j in range(2):
                    ref, base = (full[at], 2) if at < z.shards else (others[at - z.shards], 0)
                    block = ref[base + i, :, z.lanes(h)]
                    both[h, at, pl.ds(i * z.tok, z.tok), z.lanes(j)] = (
                        block if i == j else jnp.zeros_like(block)
                    )
        for h in heads:
            for i in range(3):
                stats[h, at, i : i + 1, :] = jnp.full((1, z.tok), 0.0 if i else -3e38, F32)
        for rows, needed in z.blocks(count):

            @pl.when(needed)
            def _():
                sums = softmax_sums(
                    z,
                    first,
                    count,
                    rows,
                    ranked,
                    kv,
                    [both.at[h, at] for h in heads],
                    [score.at[h, at] for h in heads],
                    [dprob.at[h, at] for h in heads],
                )
                for h in heads:
                    for i in range(3):
                        stats[h, at, i : i + 1, :] = sums[i][h]


def ahead_kernel(z, meta_ref, bias, both, stats, *refs):
    tiles, (merged, kt, vt, score, dprob, kv, ranked) = by_hop(z, refs[:3]), refs[3:]
    first = z.first_head(meta_ref)
    heads = range(z.batch)
    spans, ranks = z.ranks(meta_ref, True)
    order_tiles(z, tiles, ranks, kv, kt, vt)
    for span, rank in zip(spans, ranks):
        ranked[rank] = bias[span]
    for at, count, live in z.queries(meta_ref, True):
        merged[:, at] = stats[:, at]

        for rows, needed in z.blocks(count):

            @pl.when(needed & (live == 1))
            def _():
                far = softmax_sums(
                    z,
                    first,
                    count,
                    rows,
                    ranked,
                    kv,
                    [both.at[h, at] for h in heads],
                    [score.at[h, at] for h in heads],
                    [dprob.at[h, at] for h in heads],
                )
                sums = merge_sums([read_sums(stats, heads, at), far])
                for h in heads:
                    for i in range(3):
                        merged[h, at, i : i + 1, :] = sums[h][i]


def back_kernel(z, meta_ref, both, stats, kt, vt, score, dprob, *refs):
    others, refs = refs[: z.replicas - 1], refs[z.replicas - 1 :]
    final, ot, dqt, own_sums, sums, acc = refs
    heads = range(z.batch)
    acc[...] = jnp.zeros_like(acc)
    for at, count, live in z.queries(meta_ref, True):
        parts = [read_sums(stats, heads, at)]
        for turn, other in enumerate(others, 1):
            place = (at // z.shards - turn) % z.replicas * z.shards + at % z.shards
            parts.append(read_sums(other, heads, place))
        log_total, delta = [], []
        for h, (peak, total, mixed) in enumerate(merge_sums(parts)):
            log_total.append(peak + jnp.log2(total))
            delta.append(mixed / total)
            final[h, at, 0:1, :] = log_total[h]
            final[h, at, 1:2, :] = delta[h]

        for rows, needed in z.blocks(count):

            @pl.when(needed & (live == 1))
            def _():
                pairs = list(
                    weights(
                        z,
                        rows,
                        log_total,
                        delta,
                        [score.at[h, at] for h in heads],
                        [dprob.at[h, at] for h in heads],
                    )
                )
                add_key_gradients(rows, pairs, [both.at[h, at] for h in heads], acc)
                for h, found in enumerate(row_gradients(rows, pairs, kt, vt)):
                    ot[h, at], dqt[h, at] = found

        @pl.when((count == 0) | (live != 1))
        def _():
            ot[:, at] = jnp.zeros_like(ot[:, at])
            dqt[:, at] = jnp.zeros_like(dqt[:, at])

    goals = [own_sums] + [sums.at[i] for i in range(z.shards - 1)]
    write_sums(z, goals, z.ranks(meta_ref, True)[1], acc)


def rows_kernel(z, meta_ref, kt, vt, score, dprob, final, ot_in, dqt_in, *refs, mine):
    rows_out = refs[1:]
    heads = range(z.batch)
    for at, count, _ in z.queries(meta_ref, False):
        if mine != (at < z.shards):
            continue
        log_total = [final[h, at, 0:1, :] for h in heads]
        delta = [final[h, at, 1:2, :] for h in heads]

        def write(h, out, dq):
            goal = rows_out[at if mine else at - z.shards]
            goal[0, :, z.lanes(h)] = out.astype(BF16).T
            goal[1, :, z.lanes(h)] = (dq * z.inv_root).astype(BF16).T

        for rows, needed in z.blocks(count):

            @pl.when(needed)
            def _():
                pairs = weights(
                    z,
                    rows,
                    log_total,
                    delta,
                    [score.at[h, at] for h in heads],
                    [dprob.at[h, at] for h in heads],
                )
                for h, (out, dq) in enumerate(row_gradients(rows, pairs, kt, vt)):
                    write(h, ot_in[h, at] + out, dqt_in[h, at] + dq)

        @pl.when(count == 0)
        def _():
            for h in heads:
                write(h, ot_in[h, at], dqt_in[h, at])


def sums_kernel(z, meta_ref, both, score, dprob, final, *refs):
    sums, acc = refs[1:-1], refs[-1]
    heads = range(z.batch)
    acc[...] = jnp.zeros_like(acc)
    for at, count, _ in z.queries(meta_ref, False):
        for rows, needed in z.blocks(count):

            @pl.when(needed)
            def _():
                pairs = weights(
                    z,
                    rows,
                    [final[h, at, 0:1, :] for h in heads],
                    [final[h, at, 1:2, :] for h in heads],
                    [score.at[h, at] for h in heads],
                    [dprob.at[h, at] for h in heads],
                )
                add_key_gradients(rows, pairs, [both.at[h, at] for h in heads], acc)

    write_sums(z, sums, z.ranks(meta_ref, False)[1], acc)


def add_up(terms, at=()):
    total = terms[0][at].astype(F32)
    for term in terms[1:]:
        total = total + term[at].astype(F32)
    return total.astype(BF16)


def add(lists):
    count = len(lists[0])

    def kernel(*refs):
        for i in range(len(lists)):
            for which in range(2):
                refs[i - len(lists)][which] = add_up(refs[i * count : (i + 1) * count], which)

    operands = [x for parts in lists for x in parts]
    return pl.pallas_call(
        kernel,
        out_shape=[jax.ShapeDtypeStruct(operands[0].shape, BF16)] * len(lists),
        in_specs=[whole(VMEM)] * len(operands),
        out_specs=[whole(VMEM)] * len(lists),
        compiler_params=params(8),
        name="add",
    )(*operands)


def merge(lists, joined, last):
    count = len(lists[0])

    def kernel(*refs):
        refs, outs = refs[: -1 - len(lists)], refs[-1 - len(lists) :]
        arrived, refs = refs[0], refs[1:]
        for which in range(2):
            for i in range(len(lists)):
                terms = list(refs[i * count : (i + 1) * count]) + [arrived.at[i]]
                outs[i][which] = add_up(terms, which)
            outs[-1][which] = add_up(refs[len(lists) * count :], which)

    operands = [joined] + [x for parts in lists for x in parts] + last
    return pl.pallas_call(
        kernel,
        out_shape=[jax.ShapeDtypeStruct(last[0].shape, BF16)] * (len(lists) + 1),
        in_specs=[whole(VMEM)] * len(operands),
        out_specs=[whole(VMEM)] * (len(lists) + 1),
        compiler_params=params(8),
        name="merge",
    )(*operands)


def unpack(pos, lists):
    shards = len(lists)
    tok, cols = lists[0][0].shape[1:]

    def kernel(pos_ref, *refs):
        ins, outs = list(refs[:-2]), refs[-2:]
        for hop in range(shards):
            terms, ins = ins[: len(lists[hop])], ins[len(lists[hop]) :]
            lanes = pl.ds(pl.multiple_of((pos_ref[0] ^ hop) * cols, 128), cols)
            for i in range(2):
                outs[i][:, lanes] = add_up(terms, i)

    operands = [x for parts in lists for x in parts]
    return pl.pallas_call(
        kernel,
        out_shape=[jax.ShapeDtypeStruct((tok, cols * shards), BF16)] * 2,
        in_specs=[whole(SMEM)] + [whole(VMEM)] * len(operands),
        out_specs=[whole(VMEM)] * 2,
        compiler_params=params(8),
        name="unpack",
    )(pos, *operands)


def per_device(queries, keys, values, grad_out, span_of_group, noise_level, next_live, level_bias):
    tok, model = queries.shape
    heads = level_bias.shape[1]
    width = model // heads
    groups = lax.axis_size("tm")
    tiles = lax.axis_size("tile")
    shards = shard_count(heads, groups)
    replicas = groups // shards
    own = heads // shards
    cols = own * width
    z = Sizes(shards, replicas, tiles, own, width, tok)
    me = lax.axis_index("tm")
    pos = jnp.stack([me // replicas, me % replicas, lax.axis_index("tile")]).astype(jnp.int32)
    meta = jnp.concatenate([pos, span_of_group, noise_level, next_live])
    shape = jax.ShapeDtypeStruct

    def to_shard(x, hop, lift):
        if hop == 0 and lift == 0:
            return x
        pairs = []
        for t in range(groups):
            goal = ((t // replicas) ^ hop) * replicas + (t - lift) % replicas
            for s in range(tiles):
                pairs.append((t * tiles + s, goal * tiles + (s + lift) % tiles))
        return lax.ppermute(x, ("tm", "tile"), pairs)

    def to_replica(x, turn):
        pairs = [(t, t // replicas * replicas + (t - turn) % replicas) for t in range(groups)]
        return lax.ppermute(x, "tm", pairs)

    def with_others(parts):
        return [
            [parts[hop]]
            + [
                to_replica(parts[turn * shards + hop], replicas - turn)
                for turn in range(1, replicas)
            ]
            for hop in hops
        ]

    def swapped(tiles):
        return [to_replica(x, turn) for turn in range(1, replicas) for x in tiles]

    hops = list(range(shards))
    last = shards - 1
    packed, (pair, early) = pack(z, pos, (keys, values, queries, grad_out))
    full = [to_shard(packed[hop], hop, 0) for hop in hops]
    far_first, far_last = to_shard(pair, 0, -1), to_shard(early, 0, -1)
    bias = bias_rows(z, meta, level_bias.T, full[1])
    direct = stack(full[1:last], 0, (bias,))
    far = [far_first, to_shard(direct, 0, -1), to_shard(far_last, last, 0)]
    rows = swapped([stack(full[:1], 2, flat=True), stack(full[1:last], 2, (bias,)), stack(full[last:], 2, (far_first, far_last), True)])

    scalars = [(meta, "scalar")]
    one = shape((2, tok, cols), BF16)
    square = shape((own, width, shards * tok), BF16)
    block = shape((own, groups, shards * tok, tok), F32)
    stat = shape((own, groups, 8, tok), F32)
    part = shape((own, groups, width, tok), F32)
    batch = z.batch
    limit = 8 if batch == own else 56
    tiles_scratch = VMEM((batch, shards * tok, 2 * width), BF16)
    ranked_scratch = VMEM((shards, heads, tok), F32)
    sums_scratch = VMEM((batch, shards * tok, 2 * width), F32)
    kt, vt, both, score, dprob, stats = z.call(
        own_kernel,
        "own",
        limit,
        scalars + [(bias, "all")] + [(x, "lanes") for x in full + rows],
        [
            (square, "heads"),
            (square, "heads"),
            (shape((own, groups, 2 * tok, 2 * width), BF16), "heads"),
            (block, "heads"),
            (block, "heads"),
            (stat, "heads"),
        ],
        [tiles_scratch, ranked_scratch],
    )
    merged, far_kt, far_vt, far_score, far_dprob = z.call(
        ahead_kernel,
        "ahead",
        limit,
        scalars
        + [(bias, "all"), (both, "heads"), (stats, "heads")]
        + [(after(x, stats), "lanes") for x in far],
        [
            (stat, "heads"),
            (square, "heads"),
            (square, "heads"),
            (block, "heads"),
            (block, "heads"),
        ],
        [tiles_scratch, ranked_scratch],
    )
    final, ot, dqt, first_sums, far_sums = z.call(
        back_kernel,
        "back",
        limit,
        scalars
        + [(x, "heads") for x in (both, merged, far_kt, far_vt, far_score, far_dprob)]
        + [(x, "heads") for x in swapped([merged])],
        [
            (stat, "heads"),
            (part, "heads"),
            (part, "heads"),
            (one, "lanes"),
            (shape((last, 2, tok, cols), BF16), "lanes"),
        ],
        [sums_scratch],
    )
    far_home = to_shard(far_sums, 0, 1)
    operands = scalars + [(x, "heads") for x in (kt, vt, score, dprob, final, ot, dqt)]
    rows_others = z.call(
        functools.partial(rows_kernel, mine=False),
        "rows_others",
        limit,
        operands + [(first_sums, "lanes")],
        [(one, "lanes")] * (groups - shards),
        [],
    )
    rows_mine = z.call(
        functools.partial(rows_kernel, mine=True),
        "rows",
        limit,
        operands + [(first_sums, "lanes")],
        [(one, "lanes")] * shards,
        [],
    )
    row_sums = add(with_others([*rows_mine, *rows_others]))
    rows_home = [to_shard(row_sums[hop], hop, 0) for hop in hops[::-1]][::-1]
    near_sums = z.call(
        sums_kernel,
        "sums",
        limit,
        scalars
        + [(x, "heads") for x in (both, score, dprob, final)]
        + [(row_sums[0], "lanes")],
        [(one, "lanes")] * shards,
        [sums_scratch],
    )
    *sums, first_late = merge([[x] for x in near_sums[1:]], far_home, [first_sums])
    sums_home = [to_shard(x, hop, 0) for hop, x in zip(hops[:0:-1], sums[::-1])][::-1]
    first_home = to_shard(first_late, 0, 1)
    attended, grad_queries = unpack(pos, [[x] for x in rows_home])
    grad_keys, grad_values = unpack(
        pos, [[near_sums[0], first_home]] + [[x] for x in sums_home]
    )
    return attended, grad_queries, grad_keys, grad_values


def solution(mesh):
    sharded = P(("tm", "tile"), None)
    return jax.shard_map(
        per_device,
        mesh=mesh,
        in_specs=(sharded,) * 4 + (P(),) * 4,
        out_specs=(sharded,) * 4,
        check_vma=False,
    )
```
